32 devices in a mesh: lon: 8 (over y, x, core), lat: 4 (over z).
Axes of the slice: x: 2, y: 2, z: 4, core: 2. Of those that a mesh axis runs over, the one named last changes fastest.
Arguments:
- tracer: float32 [4096, 4096], P('lon', 'lat'), parts along dimension 1, may hold values from -7 to 7
- lower2: float32 [4096, 4096], P('lon', 'lat'), parts along dimension 1, may hold values from -4096 to -256
- lower1: float32 [4096, 4096], P('lon', 'lat'), parts along dimension 1, may hold values from -6144 to -256
- upper1: float32 [4096, 4096], P('lon', 'lat'), parts along dimension 1, may hold values from -4096 to -128
- upper2: float32 [4096, 4096], P('lon', 'lat'), parts along dimension 1, may hold values from -2048 to -64
Outputs:
- advanced: float32 [4096, 4096], P('lon', 'lat'), parts along dimension 1
The draws below stay inside these ranges and needn't reach their ends.
There are 4 independent parts, one for each index of `lat`. The reference program is written for one: setup_inputs(seed, part) draws one part's arguments, and reference() takes and returns one part's arrays. A program takes and returns all parts, laid end to end along the dimension named above; each array names one. Nothing has to cross between parts.
All inputs are finite; a program needn't handle non-finite values.
Results may differ from the reference program's by a relative error of at most 0.0003.
Values sent between devices are 32-bit elements; how exact they have to be, the bound alone decides.
A program may use at most 128 MiB of HBM per device.

```python
import math
import jax
import jax.numpy as jnp
from jax import lax

NLON = 4096
LINES = 1024
HSCALE = 2048


def coupling(key, salt, weight):
    inner_key = jax.random.fold_in(key, salt)
    key_wave, key_phase, key_rough = jax.random.split(inner_key, 3)
    position = jnp.arange(NLON, dtype=jnp.float32)[:, None] / NLON
    wave_number = jax.random.randint(key_wave, (1, LINES), 1, 4).astype(jnp.float32)
    phase_shift = jax.random.uniform(key_phase, (1, LINES), jnp.float32, 0.0, 2.0 * math.pi)
    envelope = jnp.exp(0.6 * jnp.sin(2.0 * math.pi * wave_number * position + phase_shift))
    rough_part = jax.random.uniform(key_rough, (NLON, LINES), jnp.float32, 0.6, 1.8)
    return (-(weight * HSCALE) * envelope * rough_part).astype(jnp.float32)


def draw_lower2(key, part):
    return coupling(key, 11, 0.5)


def draw_lower1(key, part):
    return coupling(key, 12, 0.7)


def draw_upper1(key, part):
    return coupling(key, 13, 0.4)


def draw_upper2(key, part):
    return coupling(key, 14, 0.2)


def draw_tracer(key, part):
    inner_key = jax.random.fold_in(key, 21)
    key_rough, key_first, key_second, phase_first, phase_second = jax.random.split(inner_key, 5)
    position = jnp.arange(NLON, dtype=jnp.float32)[:, None] / NLON
    wave_first = jax.random.randint(key_first, (1, LINES), 1, 9).astype(jnp.float32)
    wave_second = jax.random.randint(key_second, (1, LINES), 1, 9).astype(jnp.float32)
    shift_first = jax.random.uniform(phase_first, (1, LINES), jnp.float32, 0.0, 2.0 * math.pi)
    shift_second = jax.random.uniform(phase_second, (1, LINES), jnp.float32, 0.0, 2.0 * math.pi)
    smooth_part = 0.8 * jnp.sin(2.0 * math.pi * wave_first * position + shift_first) + 0.8 * jnp.sin(2.0 * math.pi * wave_second * position + shift_second)
    rough_part = jnp.clip(jax.random.normal(key_rough, (NLON, LINES), jnp.float32), -5.0, 5.0)
    return (smooth_part + rough_part).astype(jnp.float32)


def setup_inputs(seed: int = 0, part: int = 0) -> dict:
    streams_of = jax.random.split(jax.random.key(seed), 6)
    own_keys = jax.random.split(jax.random.fold_in(streams_of[5], part), 6)
    return {
        "tracer": draw_tracer(jax.random.fold_in(jax.random.fold_in(streams_of[5], part), 71), part),
        "lower2": draw_lower2(jax.random.fold_in(jax.random.fold_in(streams_of[5], part), 71), part),
        "lower1": draw_lower1(jax.random.fold_in(jax.random.fold_in(streams_of[5], part), 71), part),
        "upper1": draw_upper1(jax.random.fold_in(jax.random.fold_in(streams_of[5], part), 71), part),
        "upper2": draw_upper2(jax.random.fold_in(jax.random.fold_in(streams_of[5], part), 71), part),
    }


def reference(tracer, lower2, lower1, upper1, upper2):
    diagonal = 1.0 + (jnp.abs(lower2) + jnp.abs(lower1) + jnp.abs(upper1) + jnp.abs(upper2))
    padded = jnp.pad(tracer, ((2, 2), (0, 0)))
    applied = lower2 * padded[0:-4] + lower1 * padded[1:-3] + diagonal * tracer + upper1 * padded[3:-1] + upper2 * padded[4:]
    source = 2.0 * tracer - applied
    zero_row = jnp.zeros_like(tracer[0])

    def forward(state, row_data):
        last_p, last_q, last_g, older_p, older_q, older_g = state
        far_low, near_low, centre, near_high, far_high, target = row_data
        beta_term = near_low - far_low * older_p
        pivot_value = centre - far_low * older_q - beta_term * last_p
        new_p = (near_high - beta_term * last_q) / pivot_value
        new_q = far_high / pivot_value
        new_g = (target - far_low * older_g - beta_term * last_g) / pivot_value
        return (new_p, new_q, new_g, last_p, last_q, last_g), (new_p, new_q, new_g)

    start_state = (zero_row, zero_row, zero_row, zero_row, zero_row, zero_row)
    _, (coef_p, coef_q, coef_g) = lax.scan(forward, start_state, (lower2, lower1, diagonal, upper1, upper2, source))

    def backward(state, row_data):
        after_one, after_two = state
        factor_p, factor_q, factor_g = row_data
        solved = factor_g - factor_p * after_one - factor_q * after_two
        return (solved, after_one), solved

    _, advanced = lax.scan(backward, (zero_row, zero_row), (coef_p, coef_q, coef_g), reverse=True)
    return advanced
```

```python
import functools

import jax
import jax.numpy as jnp
from jax import lax
from jax.experimental import pallas as pl
from jax.experimental.pallas import tpu as pltpu
from jax.sharding import PartitionSpec as P

SUB = 8
LANE = 128
SENT = 24
BACK = 8
GROUP = 4
F32 = jnp.float32


def unpack(piece):
    return piece[0:2], piece[2:6], piece[6:10], piece[10:12], piece[12:16], piece[16:20]


def mat_vec(m, v):
    return (m[0] * v[0] + m[1] * v[1], m[2] * v[0] + m[3] * v[1])


def mat_mat(m, k):
    return (
        m[0] * k[0] + m[1] * k[2],
        m[0] * k[1] + m[1] * k[3],
        m[2] * k[0] + m[3] * k[2],
        m[2] * k[1] + m[3] * k[3],
    )


def plus(a, b):
    return tuple(x + y for x, y in zip(a, b))


def inverse(m):
    scale = 1.0 / (m[0] * m[3] - m[1] * m[2])
    return (m[3] * scale, -(m[1] * scale), -(m[2] * scale), m[0] * scale)


def interface(west, east, constant_only=False):
    _, _, _, lc, le, lw = unpack(west)
    fc, fe, fw, _, _, _ = unpack(east)
    loop = mat_mat(fw, le)
    inv = inverse((1.0 - loop[0], -loop[1], -loop[2], 1.0 - loop[3]))
    first_c = mat_vec(inv, plus(fc, mat_vec(fw, lc)))
    last_c = plus(lc, mat_vec(le, first_c))
    if constant_only:
        return first_c, last_c
    first_e = mat_mat(inv, fe)
    first_w = mat_mat(inv, mat_mat(fw, lw))
    last_e = mat_mat(le, first_e)
    last_w = plus(lw, mat_mat(le, first_w))
    return first_c, first_e, first_w, last_c, last_e, last_w


def joined(west, east):
    first_c, first_e, first_w, last_c, last_e, last_w = interface(west, east)
    fc, fe, fw, _, _, _ = unpack(west)
    _, _, _, lc, le, lw = unpack(east)
    return (
        plus(fc, mat_vec(fe, first_c))
        + mat_mat(fe, first_e)
        + plus(fw, mat_mat(fe, first_w))
        + plus(lc, mat_vec(lw, last_c))
        + plus(le, mat_mat(lw, last_e))
        + mat_mat(lw, last_w)
    )


EMPTY = (0.0, 0.0, 1.0, 0.0, 0.0, 1.0, 0.0, 0.0, 0.0, 0.0) + (
    0.0, 0.0, 0.0, 0.0, 0.0, 0.0, 1.0, 0.0, 0.0, 1.0)


def moved(piece, by):
    count = piece[0].shape[0]
    place = lax.broadcasted_iota(jnp.int32, piece[0].shape, 0)
    inside = place >= by if by > 0 else place < count + by
    return tuple(
        jnp.where(inside, pltpu.roll(x, by % count, 0), blank) for x, blank in zip(piece, EMPTY)
    )


def suffixes(piece):
    step = 1
    while step < piece[0].shape[0]:
        piece = joined(piece, moved(piece, -step))
        step *= 2
    return piece


def prefixes_before(piece):
    piece = moved(piece, 1)
    step = 1
    while step < piece[0].shape[0]:
        piece = joined(moved(piece, step), piece)
        step *= 2
    return piece


def kernel(
    peers, t_hbm, l2_hbm, l1_hbm, u1_hbm, u2_hbm, z_hbm,
    t_s, l2_s, l1_s, u1_s, u2_s, z_s, p_s, q_s, g_s, wa_s, wb_s,
    piece_s, inner_s, send_s, recv_s, back_s, ret_s,
    in_sem, out_sem, send_sem, recv_sem, back_send_sem, back_recv_sem,
):
    rows, lines = t_hbm.shape
    tiles = lines // LANE
    length = rows // SUB
    group = min(GROUP, tiles)
    me = lax.axis_index("lon")
    others = [lax.rem(me + k, peers) for k in range(1, peers)]

    def owning(who, action):
        if tiles < peers:
            pl.when(who < tiles)(action)
        else:
            action()

    def loads(tile):
        pairs = ((t_hbm, t_s), (l2_hbm, l2_s), (l1_hbm, l1_s), (u1_hbm, u1_s), (u2_hbm, u2_s))
        return [
            pltpu.make_async_copy(
                src.at[:, pl.ds(tile * LANE, LANE)],
                dst.at[pl.ds(tile * rows, rows), :],
                in_sem.at[idx, tile],
            )
            for idx, (src, dst) in enumerate(pairs)
        ]

    for tile in range(tiles):
        for copy in loads(tile):
            copy.start()

    barrier = pltpu.get_barrier_semaphore()
    for peer in others:
        pl.semaphore_signal(
            barrier, inc=1, device_id={"lon": peer}, device_id_type=pl.DeviceIdType.MESH
        )

    ret_s[0] = jnp.zeros((SUB, LANE), F32)
    back_s[pl.ds(0, SUB), :] = jnp.ones((SUB, LANE), F32)
    zero = ret_s[0]
    one = back_s[pl.ds(0, SUB), :]

    def strided(tile, row):
        return pl.ds(tile * rows + row, SUB, stride=length)

    def packed(tile):
        return pl.ds(tile * SUB, SUB)

    for base in range(0, tiles, group):
        members = list(range(base, base + group))
        for tile in members:
            for copy in loads(tile):
                copy.wait()

        def forward(i, state, members=members):
            new_state = []
            for tile, (p1, q1, g1, a1, b1, p2, q2, g2, a2, b2) in zip(members, state):
                here = strided(tile, i)
                l2, l1, u1, u2 = l2_s[here, :], l1_s[here, :], u1_s[here, :], u2_s[here, :]
                target = t_s[here, :]
                centre = 1.0 + (jnp.abs(l2) + jnp.abs(l1) + jnp.abs(u1) + jnp.abs(u2))
                beta = l1 - l2 * p2
                scale = 1.0 / ((centre - l2 * q2) - beta * p1)
                p0 = (u1 - beta * q1) * scale
                q0 = u2 * scale
                far = l2 * scale
                near = beta * scale
                g0 = (target * scale - far * g2) - near * g1
                a0 = -(far * a2 + near * a1)
                b0 = -(far * b2 + near * b1)
                at = packed(tile)
                p_s[i, at, :] = p0
                q_s[i, at, :] = q0
                g_s[i, at, :] = g0
                wa_s[i, at, :] = a0
                wb_s[i, at, :] = b0
                new_state.append((p0, q0, g0, a0, b0, p1, q1, g1, a1, b1))
            return tuple(new_state)

        start = (zero, zero, zero, zero, -one, zero, zero, zero, -one, zero)
        ends = lax.fori_loop(0, length, forward, (start,) * group, unroll=2)

        def first_rows(i, state, members=members):
            new_state = []
            for tile, forms in zip(members, state):
                at = packed(tile)
                p, q, g = p_s[i, at, :], q_s[i, at, :], g_s[i, at, :]
                wa, wb = wa_s[i, at, :], wb_s[i, at, :]
                new_forms = []
                for c, x, y, a, b in forms:
                    new_forms.append((c + x * g, y - x * p, -(x * q), a - x * wa, b - x * wb))
                new_state.append(tuple(new_forms))
            return tuple(new_state)

        forms = ((zero, one, zero, zero, zero), (zero, zero, one, zero, zero))
        firsts = lax.fori_loop(0, length, first_rows, (forms,) * group, unroll=2)

        for tile, end, (f0, f1) in zip(members, ends, firsts):
            p1, q1, g1, a1, b1, p2, q2, g2, a2, b2 = end
            piece = (
                f0[0], f1[0],
                f0[1], f0[2], f1[1], f1[2],
                f0[3], f0[4], f1[3], f1[4],
                g2 - p2 * g1, g1,
                p2 * p1 - q2, p2 * q1, -p1, -q1,
                p2 * a1 - a2, p2 * b1 - b2, -a1, -b1,
            )
            for idx, value in enumerate(piece):
                piece_s[tile, pl.ds(idx * SUB, SUB), :] = value

    def stored(tile):
        return tuple(piece_s[tile, pl.ds(idx * SUB, SUB), :] for idx in range(20))

    def whole(tile, carry):
        total = suffixes(stored(tile))
        for idx, value in enumerate(total):
            inner_s[tile, pl.ds(idx * SUB, SUB), :] = value
            send_s[tile, pl.ds(idx, 1), :] = value[0:1, :]
        return carry

    lax.fori_loop(0, tiles, whole, 0)

    def outward(peer, source):
        return pltpu.make_async_remote_copy(
            src_ref=send_s.at[peer],
            dst_ref=recv_s.at[pl.ds(pl.multiple_of(source * SENT, SENT), SENT), :],
            send_sem=send_sem.at[peer],
            recv_sem=recv_sem.at[source],
            device_id={"lon": peer},
            device_id_type=pl.DeviceIdType.MESH,
        )

    def homeward(peer, source):
        return pltpu.make_async_remote_copy(
            src_ref=back_s.at[pl.ds(pl.multiple_of(peer * BACK, BACK), BACK), :],
            dst_ref=ret_s.at[source],
            send_sem=back_send_sem.at[peer],
            recv_sem=back_recv_sem.at[source],
            device_id={"lon": peer},
            device_id_type=pl.DeviceIdType.MESH,
        )

    pl.semaphore_wait(barrier, peers - 1)
    for peer in others:
        owning(peer, lambda peer=peer: outward(peer, me).start())

    def inside(tile, carry):
        total = tuple(inner_s[tile, pl.ds(idx * SUB, SUB), :] for idx in range(20))
        parts = interface(prefixes_before(stored(tile)), total)
        for idx, value in enumerate(sum(parts, ())):
            inner_s[tile, pl.ds(idx * SUB, SUB), :] = value
        return carry

    lax.fori_loop(0, tiles, inside, 0)

    def solve_lines():
        recv_s[pl.ds(pl.multiple_of(me * SENT, SENT), SENT), :] = send_s[me]
        for peer in others:
            outward(me, peer).wait_recv()
        segments = tuple(recv_s[pl.ds(idx, peers, stride=SENT), :] for idx in range(20))
        first, last = interface(prefixes_before(segments), suffixes(segments), True)
        place = lax.broadcasted_iota(jnp.int32, (peers, LANE), 0)
        east = [jnp.where(place < peers - 1, pltpu.roll(x, peers - 1, 0), 0.0) for x in first]
        west = [jnp.where(place > 0, x, 0.0) for x in last]
        for idx, value in enumerate(east + west):
            back_s[pl.ds(idx, peers, stride=BACK), :] = value
        for peer in others:
            homeward(peer, me).start()
        ret_s[me] = back_s[pl.ds(pl.multiple_of(me * BACK, BACK), BACK), :]

    owning(me, solve_lines)

    for peer in others:
        owning(peer, lambda peer=peer: homeward(me, peer).wait_recv())

    place = lax.broadcasted_iota(jnp.int32, (SUB, LANE), 0)

    def store(tile):
        return pltpu.make_async_copy(
            z_s.at[pl.ds(tile * rows, rows), :],
            z_hbm.at[:, pl.ds(tile * LANE, LANE)],
            out_sem.at[tile],
        )

    for base in range(0, tiles, group):
        members = list(range(base, base + group))
        start, bounds = [], []
        for tile in members:
            e0, e1, w0, w1 = (
                jnp.broadcast_to(ret_s[tile, pl.ds(idx, 1), :], (SUB, LANE)) for idx in range(4)
            )
            inner = tuple(inner_s[tile, pl.ds(idx * SUB, SUB), :] for idx in range(20))
            first = plus(plus(inner[0:2], mat_vec(inner[2:6], (e0, e1))), mat_vec(inner[6:10], (w0, w1)))
            last = plus(plus(inner[10:12], mat_vec(inner[12:16], (e0, e1))), mat_vec(inner[16:20], (w0, w1)))
            east = [
                jnp.where(place < SUB - 1, pltpu.roll(x, SUB - 1, 0), edge)
                for x, edge in zip(first, (e0, e1))
            ]
            start.append((east[0], east[1]))
            bounds.append(last)

        def backward(step, state, members=members, bounds=bounds):
            i = length - 1 - step
            new_state = []
            for tile, (wa, wb), (x1, x2) in zip(members, bounds, state):
                at = packed(tile)
                free = (g_s[i, at, :] - wa_s[i, at, :] * wa) - wb_s[i, at, :] * wb
                x0 = (free - q_s[i, at, :] * x2) - p_s[i, at, :] * x1
                z_s[strided(tile, i), :] = x0
                new_state.append((x0, x1))
            return tuple(new_state)

        lax.fori_loop(0, length, backward, tuple(start), unroll=2)
        for tile in members:
            store(tile).start()

    for tile in range(tiles):
        store(tile).wait()
    for peer in others:
        owning(peer, lambda peer=peer: outward(peer, me).wait_send())

    def sent_home():
        for peer in others:
            homeward(peer, me).wait_send()

    owning(me, sent_home)


def per_device(tracer, lower2, lower1, upper1, upper2):
    rows, lines = tracer.shape
    peers = lax.axis_size("lon")
    tiles = lines // LANE
    assert rows % (2 * SUB) == 0 and lines % LANE == 0 and tiles <= peers
    assert tiles % min(GROUP, tiles) == 0
    plane = pltpu.VMEM((tiles * rows, LANE), F32)
    factor = pltpu.VMEM((rows // SUB, tiles * SUB, LANE), F32)
    sem = pltpu.SemaphoreType.DMA
    solved = pl.pallas_call(
        functools.partial(kernel, peers),
        out_shape=jax.ShapeDtypeStruct((rows, lines), F32),
        in_specs=[pl.BlockSpec(memory_space=pl.ANY)] * 5,
        out_specs=pl.BlockSpec(memory_space=pl.ANY),
        scratch_shapes=[plane] * 6
        + [factor] * 5
        + [
            pltpu.VMEM((tiles, 20 * SUB, LANE), F32),
            pltpu.VMEM((tiles, 20 * SUB, LANE), F32),
            pltpu.VMEM((tiles, SENT, LANE), F32),
            pltpu.VMEM((peers * SENT, LANE), F32),
            pltpu.VMEM((peers * BACK, LANE), F32),
            pltpu.VMEM((tiles, BACK, LANE), F32),
            sem((5, tiles)),
            sem((tiles,)),
            sem((peers,)),
            sem((peers,)),
            sem((peers,)),
            sem((peers,)),
        ],
        compiler_params=pltpu.CompilerParams(
            collective_id=0, has_side_effects=True, vmem_limit_bytes=48 * 1024 * 1024
        ),
        cost_estimate=pl.CostEstimate(
            flops=90 * rows * lines, bytes_accessed=24 * rows * lines, transcendentals=0
        ),
    )(tracer, lower2, lower1, upper1, upper2)
    return 2.0 * solved - tracer


def solution(mesh):
    spec = P("lon", "lat")
    return jax.shard_map(
        per_device, mesh=mesh, in_specs=(spec,) * 5, out_specs=spec, check_vma=False
    )
```

```python
import functools

import jax
import jax.numpy as jnp
from jax import lax
from jax.experimental import pallas as pl
from jax.experimental.pallas import tpu as pltpu
from jax.sharding import PartitionSpec as P

SUB = 8
LANE = 128
SENT = 24
BACK = 8
GROUP = 4
F32 = jnp.float32


def unpack(piece):
    return piece[0:2], piece[2:6], piece[6:10], piece[10:12], piece[12:16], piece[16:20]


def mat_vec(m, v):
    return (m[0] * v[0] + m[1] * v[1], m[2] * v[0] + m[3] * v[1])


def mat_mat(m, k):
    return (
        m[0] * k[0] + m[1] * k[2],
        m[0] * k[1] + m[1] * k[3],
        m[2] * k[0] + m[3] * k[2],
        m[2] * k[1] + m[3] * k[3],
    )


def plus(a, b):
    return tuple(x + y for x, y in zip(a, b))


def inverse(m):
    scale = 1.0 / (m[0] * m[3] - m[1] * m[2])
    return (m[3] * scale, -(m[1] * scale), -(m[2] * scale), m[0] * scale)


def interface(west, east, constant_only=False):
    _, _, _, lc, le, lw = unpack(west)
    fc, fe, fw, _, _, _ = unpack(east)
    loop = mat_mat(fw, le)
    inv = inverse((1.0 - loop[0], -loop[1], -loop[2], 1.0 - loop[3]))
    first_c = mat_vec(inv, plus(fc, mat_vec(fw, lc)))
    last_c = plus(lc, mat_vec(le, first_c))
    if constant_only:
        return first_c, last_c
    first_e = mat_mat(inv, fe)
    first_w = mat_mat(inv, mat_mat(fw, lw))
    last_e = mat_mat(le, first_e)
    last_w = plus(lw, mat_mat(le, first_w))
    return first_c, first_e, first_w, last_c, last_e, last_w


def joined(west, east):
    first_c, first_e, first_w, last_c, last_e, last_w = interface(west, east)
    fc, fe, fw, _, _, _ = unpack(west)
    _, _, _, lc, le, lw = unpack(east)
    return (
        plus(fc, mat_vec(fe, first_c))
        + mat_mat(fe, first_e)
        + plus(fw, mat_mat(fe, first_w))
        + plus(lc, mat_vec(lw, last_c))
        + plus(le, mat_mat(lw, last_e))
        + mat_mat(lw, last_w)
    )


EMPTY = (0.0, 0.0, 1.0, 0.0, 0.0, 1.0, 0.0, 0.0, 0.0, 0.0) + (
    0.0, 0.0, 0.0, 0.0, 0.0, 0.0, 1.0, 0.0, 0.0, 1.0)


def moved(piece, by):
    count = piece[0].shape[0]
    place = lax.broadcasted_iota(jnp.int32, piece[0].shape, 0)
    inside = place >= by if by > 0 else place < count + by
    return tuple(
        jnp.where(inside, pltpu.roll(x, by % count, 0), blank) for x, blank in zip(piece, EMPTY)
    )


def suffixes(piece):
    step = 1
    while step < piece[0].shape[0]:
        piece = joined(piece, moved(piece, -step))
        step *= 2
    return piece


def prefixes_before(piece):
    piece = moved(piece, 1)
    step = 1
    while step < piece[0].shape[0]:
        piece = joined(moved(piece, step), piece)
        step *= 2
    return piece


def kernel(
    peers, t_hbm, l2_hbm, l1_hbm, u1_hbm, u2_hbm, z_hbm,
    t_s, l2_s, l1_s, u1_s, u2_s, z_s, p_s, q_s, g_s, wa_s, wb_s,
    piece_s, inner_s, send_s, recv_s, back_s, ret_s,
    in_sem, out_sem, send_sem, recv_sem, back_send_sem, back_recv_sem,
):
    _, length, lines = t_hbm.shape
    tiles = lines // LANE
    pitch = t_s.shape[1]
    group = min(GROUP, tiles)
    me = lax.axis_index("lon")
    others = [lax.rem(me + k, peers) for k in range(1, peers)]

    def owning(who, action):
        if tiles < peers:
            pl.when(who < tiles)(action)
        else:
            action()

    def loads(tile):
        pairs = ((t_hbm, t_s), (l2_hbm, l2_s), (l1_hbm, l1_s), (u1_hbm, u1_s), (u2_hbm, u2_s))
        return [
            pltpu.make_async_copy(
                src.at[:, :, pl.ds(tile * LANE, LANE)],
                dst.at[pl.ds(tile * SUB, SUB), pl.ds(0, length), :],
                in_sem.at[idx, tile],
            )
            for idx, (src, dst) in enumerate(pairs)
        ]

    flat_rows = tiles * SUB * pitch
    t_f, l2_f, l1_f, u1_f, u2_f, z_f = (
        ref.reshape(flat_rows, LANE) for ref in (t_s, l2_s, l1_s, u1_s, u2_s, z_s)
    )

    for tile in range(tiles):
        for copy in loads(tile):
            copy.start()

    barrier = pltpu.get_barrier_semaphore()
    for peer in others:
        pl.semaphore_signal(
            barrier, inc=1, device_id={"lon": peer}, device_id_type=pl.DeviceIdType.MESH
        )

    ret_s[0] = jnp.zeros((SUB, LANE), F32)
    back_s[pl.ds(0, SUB), :] = jnp.ones((SUB, LANE), F32)
    zero = ret_s[0]
    one = back_s[pl.ds(0, SUB), :]

    def strided(tile, row):
        return pl.ds(tile * SUB * pitch + row, SUB, stride=pitch)

    def packed(tile):
        return pl.ds(tile * SUB, SUB)

    for base in range(0, tiles, group):
        members = list(range(base, base + group))
        for tile in members:
            for copy in loads(tile):
                copy.wait()

        def forward(i, state, members=members):
            new_state = []
            for tile, (p1, q1, g1, a1, b1, p2, q2, g2, a2, b2) in zip(members, state):
                here = strided(tile, i)
                l2, l1, u1, u2 = l2_f[here, :], l1_f[here, :], u1_f[here, :], u2_f[here, :]
                target = t_f[here, :]
                centre = 1.0 + (jnp.abs(l2) + jnp.abs(l1) + jnp.abs(u1) + jnp.abs(u2))
                beta = l1 - l2 * p2
                scale = pl.reciprocal((centre - l2 * q2) - beta * p1, approx=True)
                p0 = (u1 - beta * q1) * scale
                q0 = u2 * scale
                far = l2 * scale
                near = beta * scale
                g0 = (target * scale - far * g2) - near * g1
                a0 = -(far * a2 + near * a1)
                b0 = -(far * b2 + near * b1)
                at = packed(tile)
                p_s[i, at, :] = p0
                q_s[i, at, :] = q0
                g_s[i, at, :] = g0
                wa_s[i, at, :] = a0
                wb_s[i, at, :] = b0
                new_state.append((p0, q0, g0, a0, b0, p1, q1, g1, a1, b1))
            return tuple(new_state)

        start = (zero, zero, zero, zero, -one, zero, zero, zero, -one, zero)
        ends = lax.fori_loop(0, length, forward, (start,) * group, unroll=2)

        def first_rows(i, state, members=members):
            new_state = []
            for tile, forms in zip(members, state):
                at = packed(tile)
                p, q, g = p_s[i, at, :], q_s[i, at, :], g_s[i, at, :]
                wa, wb = wa_s[i, at, :], wb_s[i, at, :]
                new_forms = []
                for c, x, y, a, b in forms:
                    new_forms.append((c + x * g, y - x * p, -(x * q), a - x * wa, b - x * wb))
                new_state.append(tuple(new_forms))
            return tuple(new_state)

        forms = ((zero, one, zero, zero, zero), (zero, zero, one, zero, zero))
        firsts = lax.fori_loop(0, length, first_rows, (forms,) * group, unroll=2)

        for tile, end, (f0, f1) in zip(members, ends, firsts):
            p1, q1, g1, a1, b1, p2, q2, g2, a2, b2 = end
            piece = (
                f0[0], f1[0],
                f0[1], f0[2], f1[1], f1[2],
                f0[3], f0[4], f1[3], f1[4],
                g2 - p2 * g1, g1,
                p2 * p1 - q2, p2 * q1, -p1, -q1,
                p2 * a1 - a2, p2 * b1 - b2, -a1, -b1,
            )
            for idx, value in enumerate(piece):
                piece_s[tile, pl.ds(idx * SUB, SUB), :] = value

    def stored(tile):
        return tuple(piece_s[tile, pl.ds(idx * SUB, SUB), :] for idx in range(20))

    def whole(tile, carry):
        total = suffixes(stored(tile))
        for idx, value in enumerate(total):
            inner_s[tile, pl.ds(idx * SUB, SUB), :] = value
            send_s[tile, pl.ds(idx, 1), :] = value[0:1, :]
        return carry

    lax.fori_loop(0, tiles, whole, 0, unroll=2)

    def outward(peer, source):
        return pltpu.make_async_remote_copy(
            src_ref=send_s.at[peer],
            dst_ref=recv_s.at[pl.ds(pl.multiple_of(source * SENT, SENT), SENT), :],
            send_sem=send_sem.at[peer],
            recv_sem=recv_sem.at[source],
            device_id={"lon": peer},
            device_id_type=pl.DeviceIdType.MESH,
        )

    def homeward(peer, source):
        return pltpu.make_async_remote_copy(
            src_ref=back_s.at[pl.ds(pl.multiple_of(peer * BACK, BACK), BACK), :],
            dst_ref=ret_s.at[source],
            send_sem=back_send_sem.at[peer],
            recv_sem=back_recv_sem.at[source],
            device_id={"lon": peer},
            device_id_type=pl.DeviceIdType.MESH,
        )

    pl.semaphore_wait(barrier, peers - 1)
    for peer in others:
        owning(peer, lambda peer=peer: outward(peer, me).start())

    def inside(tile, carry):
        total = tuple(inner_s[tile, pl.ds(idx * SUB, SUB), :] for idx in range(20))
        parts = interface(prefixes_before(stored(tile)), total)
        for idx, value in enumerate(sum(parts, ())):
            inner_s[tile, pl.ds(idx * SUB, SUB), :] = value
        return carry

    lax.fori_loop(0, tiles, inside, 0, unroll=2)

    def solve_lines():
        recv_s[pl.ds(pl.multiple_of(me * SENT, SENT), SENT), :] = send_s[me]
        for peer in others:
            outward(me, peer).wait_recv()
        segments = tuple(recv_s[pl.ds(idx, peers, stride=SENT), :] for idx in range(20))
        first, last = interface(prefixes_before(segments), suffixes(segments), True)
        place = lax.broadcasted_iota(jnp.int32, (peers, LANE), 0)
        east = [jnp.where(place < peers - 1, pltpu.roll(x, peers - 1, 0), 0.0) for x in first]
        west = [jnp.where(place > 0, x, 0.0) for x in last]
        for idx, value in enumerate(east + west):
            back_s[pl.ds(idx, peers, stride=BACK), :] = value
        for peer in others:
            homeward(peer, me).start()
        ret_s[me] = back_s[pl.ds(pl.multiple_of(me * BACK, BACK), BACK), :]

    owning(me, solve_lines)

    for peer in others:
        owning(peer, lambda peer=peer: homeward(me, peer).wait_recv())

    place = lax.broadcasted_iota(jnp.int32, (SUB, LANE), 0)

    def store(tile):
        return pltpu.make_async_copy(
            z_s.at[pl.ds(tile * SUB, SUB), pl.ds(0, length), :],
            z_hbm.at[:, :, pl.ds(tile * LANE, LANE)],
            out_sem.at[tile],
        )

    for base in range(0, tiles, group):
        members = list(range(base, base + group))
        start, bounds = [], []
        for tile in members:
            e0, e1, w0, w1 = (
                jnp.broadcast_to(ret_s[tile, pl.ds(idx, 1), :], (SUB, LANE)) for idx in range(4)
            )
            inner = tuple(inner_s[tile, pl.ds(idx * SUB, SUB), :] for idx in range(20))
            first = plus(plus(inner[0:2], mat_vec(inner[2:6], (e0, e1))), mat_vec(inner[6:10], (w0, w1)))
            last = plus(plus(inner[10:12], mat_vec(inner[12:16], (e0, e1))), mat_vec(inner[16:20], (w0, w1)))
            east = [
                jnp.where(place < SUB - 1, pltpu.roll(x, SUB - 1, 0), edge)
                for x, edge in zip(first, (e0, e1))
            ]
            start.append((east[0], east[1]))
            bounds.append(last)

        def backward(step, state, members=members, bounds=bounds):
            i = length - 1 - step
            new_state = []
            for tile, (wa, wb), (x1, x2) in zip(members, bounds, state):
                at = packed(tile)
                free = (g_s[i, at, :] - wa_s[i, at, :] * wa) - wb_s[i, at, :] * wb
                x0 = (free - q_s[i, at, :] * x2) - p_s[i, at, :] * x1
                z_f[strided(tile, i), :] = 2.0 * x0 - t_f[strided(tile, i), :]
                new_state.append((x0, x1))
            return tuple(new_state)

        lax.fori_loop(0, length, backward, tuple(start), unroll=2)
        for tile in members:
            store(tile).start()

    for tile in range(tiles):
        store(tile).wait()
    for peer in others:
        owning(peer, lambda peer=peer: outward(peer, me).wait_send())

    def sent_home():
        for peer in others:
            homeward(peer, me).wait_send()

    owning(me, sent_home)


def per_device(tracer, lower2, lower1, upper1, upper2):
    rows, lines = tracer.shape
    peers = lax.axis_size("lon")
    tiles = lines // LANE
    assert rows % (SUB * SUB) == 0 and lines % LANE == 0 and tiles <= peers
    assert tiles % min(GROUP, tiles) == 0
    length = rows // SUB
    pitch = length if length % (2 * SUB) else length + SUB
    plane = pltpu.VMEM((tiles * SUB, pitch, LANE), F32)
    factor = pltpu.VMEM((length, tiles * SUB, LANE), F32)
    sem = pltpu.SemaphoreType.DMA
    solved = pl.pallas_call(
        functools.partial(kernel, peers),
        out_shape=jax.ShapeDtypeStruct((SUB, length, lines), F32),
        in_specs=[pl.BlockSpec(memory_space=pl.ANY)] * 5,
        out_specs=pl.BlockSpec(memory_space=pl.ANY),
        scratch_shapes=[plane] * 6
        + [factor] * 5
        + [
            pltpu.VMEM((tiles, 20 * SUB, LANE), F32),
            pltpu.VMEM((tiles, 20 * SUB, LANE), F32),
            pltpu.VMEM((tiles, SENT, LANE), F32),
            pltpu.VMEM((peers * SENT, LANE), F32),
            pltpu.VMEM((peers * BACK, LANE), F32),
            pltpu.VMEM((tiles, BACK, LANE), F32),
            sem((5, tiles)),
            sem((tiles,)),
            sem((peers,)),
            sem((peers,)),
            sem((peers,)),
            sem((peers,)),
        ],
        compiler_params=pltpu.CompilerParams(
            collective_id=0, has_side_effects=True, vmem_limit_bytes=60 * 1024 * 1024
        ),
        cost_estimate=pl.CostEstimate(
            flops=90 * rows * lines, bytes_accessed=24 * rows * lines, transcendentals=0
        ),
    )(*(x.reshape(SUB, length, lines) for x in (tracer, lower2, lower1, upper1, upper2)))
    return solved.reshape(rows, lines)


def solution(mesh):
    spec = P("lon", "lat")
    return jax.shard_map(
        per_device, mesh=mesh, in_specs=(spec,) * 5, out_specs=spec, check_vma=False
    )
```

```python
import functools

import jax
import jax.numpy as jnp
from jax import lax
from jax.experimental import pallas as pl
from jax.experimental.pallas import tpu as pltpu
from jax.sharding import PartitionSpec as P

SUB = 8
LANE = 128
SENT = 24
BACK = 8
GROUP = 4
PARTS = 2
LEVELS = 3
F32 = jnp.float32


def unpack(piece):
    return piece[0:2], piece[2:6], piece[6:10], piece[10:12], piece[12:16], piece[16:20]


def mat_vec(m, v):
    return (m[0] * v[0] + m[1] * v[1], m[2] * v[0] + m[3] * v[1])


def mat_mat(m, k):
    return (
        m[0] * k[0] + m[1] * k[2],
        m[0] * k[1] + m[1] * k[3],
        m[2] * k[0] + m[3] * k[2],
        m[2] * k[1] + m[3] * k[3],
    )


def plus(a, b):
    return tuple(x + y for x, y in zip(a, b))


def inverse(m):
    scale = 1.0 / (m[0] * m[3] - m[1] * m[2])
    return (m[3] * scale, -(m[1] * scale), -(m[2] * scale), m[0] * scale)


def interface(west, east, constant_only=False):
    _, _, _, lc, le, lw = unpack(west)
    fc, fe, fw, _, _, _ = unpack(east)
    loop = mat_mat(fw, le)
    inv = inverse((1.0 - loop[0], -loop[1], -loop[2], 1.0 - loop[3]))
    first_c = mat_vec(inv, plus(fc, mat_vec(fw, lc)))
    last_c = plus(lc, mat_vec(le, first_c))
    if constant_only:
        return first_c, last_c
    first_e = mat_mat(inv, fe)
    first_w = mat_mat(inv, mat_mat(fw, lw))
    last_e = mat_mat(le, first_e)
    last_w = plus(lw, mat_mat(le, first_w))
    return first_c, first_e, first_w, last_c, last_e, last_w


def joined(west, east):
    meet = interface(west, east)
    first_c, first_e, first_w, last_c, last_e, last_w = meet
    fc, fe, fw, _, _, _ = unpack(west)
    _, _, _, lc, le, lw = unpack(east)
    piece = (
        plus(fc, mat_vec(fe, first_c))
        + mat_mat(fe, first_e)
        + plus(fw, mat_mat(fe, first_w))
        + plus(lc, mat_vec(lw, last_c))
        + plus(le, mat_mat(lw, last_e))
        + mat_mat(lw, last_w)
    )
    return piece, sum(meet, ())


def rolled(values, by):
    count = values[0].shape[0]
    return tuple(pltpu.roll(x, by % count, 0) for x in values)


def split_pairs(meet, east, west, step):
    first = plus(plus(meet[0:2], mat_vec(meet[2:6], east)), mat_vec(meet[6:10], west))
    last = plus(plus(meet[10:12], mat_vec(meet[12:16], east)), mat_vec(meet[16:20], west))
    count = first[0].shape[0]
    place = lax.broadcasted_iota(jnp.int32, first[0].shape, 0)
    lower = lax.rem(place, 2 * step) < step
    if 2 * step < count:
        east = rolled(east, step)
    moved = rolled(last, step)
    return (
        tuple(jnp.where(lower, a, b) for a, b in zip(first, east)),
        tuple(jnp.where(lower, a, b) for a, b in zip(west, moved)),
    )


def kernel(
    peers, t_hbm, l2_hbm, l1_hbm, u1_hbm, u2_hbm, z_hbm,
    t_s, l2_s, l1_s, u1_s, u2_s, z_s, p_s, q_s, g_s, wa_s, wb_s,
    piece_s, inner_s, send_s, recv_s, back_s, ret_s,
    in_sem, out_sem, send_sem, recv_sem, back_send_sem, back_recv_sem,
):
    _, length, lines = t_hbm.shape
    tiles = lines // LANE
    pitch = t_s.shape[1]
    group = min(GROUP, tiles)
    me = lax.axis_index("lon")
    others = [lax.rem(me + k, peers) for k in range(1, peers)]

    def owning(who, action):
        if tiles < peers:
            pl.when(who < tiles)(action)
        else:
            action()

    def loads(tile, part):
        pairs = ((t_hbm, t_s), (l2_hbm, l2_s), (l1_hbm, l1_s), (u1_hbm, u1_s), (u2_hbm, u2_s))
        some = pl.ds(part * (length // PARTS), length // PARTS)
        return [
            pltpu.make_async_copy(
                src.at[:, some, pl.ds(tile * LANE, LANE)],
                dst.at[pl.ds(tile * SUB, SUB), some, :],
                in_sem.at[idx, tile, part],
            )
            for idx, (src, dst) in enumerate(pairs)
        ]

    flat_rows = tiles * SUB * pitch
    t_f, l2_f, l1_f, u1_f, u2_f, z_f = (
        ref.reshape(flat_rows, LANE) for ref in (t_s, l2_s, l1_s, u1_s, u2_s, z_s)
    )

    for base in range(0, tiles, group):
        for part in range(PARTS):
            for tile in range(base, base + group):
                for copy in loads(tile, part):
                    copy.start()

    barrier = pltpu.get_barrier_semaphore()
    for peer in others:
        pl.semaphore_signal(
            barrier, inc=1, device_id={"lon": peer}, device_id_type=pl.DeviceIdType.MESH
        )

    ret_s[0] = jnp.zeros((SUB, LANE), F32)
    back_s[pl.ds(0, SUB), :] = jnp.ones((SUB, LANE), F32)
    zero = ret_s[0]
    one = back_s[pl.ds(0, SUB), :]

    def strided(tile, row):
        return pl.ds(tile * SUB * pitch + row, SUB, stride=pitch)

    def packed(tile):
        return pl.ds(tile * SUB, SUB)

    for base in range(0, tiles, group):
        members = list(range(base, base + group))
        def forward(i, state, members=members):
            new_state = []
            for tile, (p1, q1, g1, a1, b1, p2, q2, g2, a2, b2) in zip(members, state):
                here = strided(tile, i)
                l2, l1, u1, u2 = l2_f[here, :], l1_f[here, :], u1_f[here, :], u2_f[here, :]
                target = t_f[here, :]
                centre = (l2 + l1 + u1 + u2) - 1.0
                beta = l1 + l2 * p2
                scale = pl.reciprocal((centre - l2 * q2) - beta * p1, approx=True)
                p0 = (u1 + beta * q1) * scale
                q0 = u2 * scale
                far = l2 * scale
                near = beta * scale
                g0 = (far * g2 - target * scale) + near * g1
                a0 = far * a2 + near * a1
                b0 = far * b2 + near * b1
                at = packed(tile)
                p_s[i, at, :] = p0
                q_s[i, at, :] = q0
                g_s[i, at, :] = g0
                wa_s[i, at, :] = a0
                wb_s[i, at, :] = b0
                new_state.append((p0, q0, g0, a0, b0, p1, q1, g1, a1, b1))
            return tuple(new_state)

        start = (zero, zero, zero, zero, one, zero, zero, zero, one, zero)
        ends = (start,) * group
        for part in range(PARTS):
            for tile in members:
                for copy in loads(tile, part):
                    copy.wait()
            span = length // PARTS
            ends = lax.fori_loop(part * span, (part + 1) * span, forward, ends, unroll=2)

        def first_rows(i, state, members=members):
            new_state = []
            for tile, forms in zip(members, state):
                at = packed(tile)
                p, q, g = p_s[i, at, :], q_s[i, at, :], g_s[i, at, :]
                wa, wb = wa_s[i, at, :], wb_s[i, at, :]
                new_forms = []
                for c, x, y, a, b in forms:
                    new_forms.append((c + x * g, y + x * p, x * q, a + x * wa, b + x * wb))
                new_state.append(tuple(new_forms))
            return tuple(new_state)

        forms = ((zero, one, zero, zero, zero), (zero, zero, one, zero, zero))
        firsts = lax.fori_loop(0, length, first_rows, (forms,) * group, unroll=2)

        for tile, end, (f0, f1) in zip(members, ends, firsts):
            p1, q1, g1, a1, b1, p2, q2, g2, a2, b2 = end
            piece = (
                f0[0], f1[0],
                f0[1], f0[2], f1[1], f1[2],
                f0[3], f0[4], f1[3], f1[4],
                g2 + p2 * g1, g1,
                p2 * p1 + q2, p2 * q1, p1, q1,
                p2 * a1 + a2, p2 * b1 + b2, a1, b1,
            )
            for idx, value in enumerate(piece):
                piece_s[tile, pl.ds(idx * SUB, SUB), :] = value

    def whole(tile, carry):
        piece = tuple(piece_s[tile, pl.ds(idx * SUB, SUB), :] for idx in range(20))
        for level in range(LEVELS):
            piece, meet = joined(piece, rolled(piece, -(1 << level)))
            for idx, value in enumerate(meet):
                inner_s[tile, pl.ds((level * 20 + idx) * SUB, SUB), :] = value
        for idx, value in enumerate(piece):
            send_s[tile, pl.ds(idx, 1), :] = value[0:1, :]
        return carry

    lax.fori_loop(0, tiles, whole, 0, unroll=2)

    def outward(peer, source):
        return pltpu.make_async_remote_copy(
            src_ref=send_s.at[peer],
            dst_ref=recv_s.at[pl.ds(pl.multiple_of(source * SENT, SENT), SENT), :],
            send_sem=send_sem.at[peer],
            recv_sem=recv_sem.at[source],
            device_id={"lon": peer},
            device_id_type=pl.DeviceIdType.MESH,
        )

    def homeward(peer, source):
        return pltpu.make_async_remote_copy(
            src_ref=back_s.at[pl.ds(pl.multiple_of(peer * BACK, BACK), BACK), :],
            dst_ref=ret_s.at[source],
            send_sem=back_send_sem.at[peer],
            recv_sem=back_recv_sem.at[source],
            device_id={"lon": peer},
            device_id_type=pl.DeviceIdType.MESH,
        )

    pl.semaphore_wait(barrier, peers - 1)
    for peer in others:
        owning(peer, lambda peer=peer: outward(peer, me).start())

    def solve_lines():
        recv_s[pl.ds(pl.multiple_of(me * SENT, SENT), SENT), :] = send_s[me]
        for peer in others:
            outward(me, peer).wait_recv()
        piece = tuple(recv_s[pl.ds(idx, peers, stride=SENT), :] for idx in range(20))
        meets = []
        step = 1
        while 2 * step < peers:
            piece, meet = joined(piece, rolled(piece, -step))
            meets.append(meet)
            step *= 2
        first, last = interface(piece, rolled(piece, -step), True)
        place = lax.broadcasted_iota(jnp.int32, (peers, LANE), 0)
        east = tuple(jnp.where(place < step, x, 0.0) for x in first)
        west = tuple(jnp.where(place < step, 0.0, x) for x in rolled(last, step))
        for meet in reversed(meets):
            step //= 2
            east, west = split_pairs(meet, east, west, step)
        for idx, value in enumerate(east + west):
            back_s[pl.ds(idx, peers, stride=BACK), :] = value
        for peer in others:
            homeward(peer, me).start()
        ret_s[me] = back_s[pl.ds(pl.multiple_of(me * BACK, BACK), BACK), :]

    owning(me, solve_lines)

    for peer in others:
        owning(peer, lambda peer=peer: homeward(me, peer).wait_recv())

    def store(tile):
        return pltpu.make_async_copy(
            z_s.at[pl.ds(tile * SUB, SUB), pl.ds(0, length), :],
            z_hbm.at[:, :, pl.ds(tile * LANE, LANE)],
            out_sem.at[tile],
        )

    for base in range(0, tiles, group):
        members = list(range(base, base + group))
        start, bounds = [], []
        for tile in members:
            e0, e1, w0, w1 = (
                jnp.broadcast_to(ret_s[tile, pl.ds(idx, 1), :], (SUB, LANE)) for idx in range(4)
            )
            east, west = (e0, e1), (w0, w1)
            for level in reversed(range(LEVELS)):
                meet = tuple(
                    inner_s[tile, pl.ds((level * 20 + idx) * SUB, SUB), :] for idx in range(20)
                )
                east, west = split_pairs(meet, east, west, 1 << level)
            start.append(east)
            bounds.append(west)

        def backward(step, state, members=members, bounds=bounds):
            i = length - 1 - step
            new_state = []
            for tile, (wa, wb), (x1, x2) in zip(members, bounds, state):
                at = packed(tile)
                free = (g_s[i, at, :] + wa_s[i, at, :] * wa) + wb_s[i, at, :] * wb
                x0 = (free + q_s[i, at, :] * x2) + p_s[i, at, :] * x1
                z_f[strided(tile, i), :] = 2.0 * x0 - t_f[strided(tile, i), :]
                new_state.append((x0, x1))
            return tuple(new_state)

        lax.fori_loop(0, length, backward, tuple(start), unroll=2)
        for tile in members:
            store(tile).start()

    for tile in range(tiles):
        store(tile).wait()
    for peer in others:
        owning(peer, lambda peer=peer: outward(peer, me).wait_send())

    def sent_home():
        for peer in others:
            homeward(peer, me).wait_send()

    owning(me, sent_home)


def per_device(tracer, lower2, lower1, upper1, upper2):
    rows, lines = tracer.shape
    peers = lax.axis_size("lon")
    tiles = lines // LANE
    assert rows % (PARTS * SUB * SUB) == 0 and peers & (peers - 1) == 0 and lines % LANE == 0 and tiles <= peers
    assert tiles % min(GROUP, tiles) == 0
    length = rows // SUB
    pitch = length if length % (2 * SUB) else length + SUB
    plane = pltpu.VMEM((tiles * SUB, pitch, LANE), F32)
    factor = pltpu.VMEM((length, tiles * SUB, LANE), F32)
    sem = pltpu.SemaphoreType.DMA
    solved = pl.pallas_call(
        functools.partial(kernel, peers),
        out_shape=jax.ShapeDtypeStruct((SUB, length, lines), F32),
        in_specs=[pl.BlockSpec(memory_space=pl.ANY)] * 5,
        out_specs=pl.BlockSpec(memory_space=pl.ANY),
        scratch_shapes=[plane] * 6
        + [factor] * 5
        + [
            pltpu.VMEM((tiles, 20 * SUB, LANE), F32),
            pltpu.VMEM((tiles, LEVELS * 20 * SUB, LANE), F32),
            pltpu.VMEM((tiles, SENT, LANE), F32),
            pltpu.VMEM((peers * SENT, LANE), F32),
            pltpu.VMEM((peers * BACK, LANE), F32),
            pltpu.VMEM((tiles, BACK, LANE), F32),
            sem((5, tiles, PARTS)),
            sem((tiles,)),
            sem((peers,)),
            sem((peers,)),
            sem((peers,)),
            sem((peers,)),
        ],
        compiler_params=pltpu.CompilerParams(
            collective_id=0, has_side_effects=True, vmem_limit_bytes=50 * 1024 * 1024
        ),
        cost_estimate=pl.CostEstimate(
            flops=90 * rows * lines, bytes_accessed=24 * rows * lines, transcendentals=0
        ),
    )(*(x.reshape(SUB, length, lines) for x in (tracer, lower2, lower1, upper1, upper2)))
    return solved.reshape(rows, lines)


def solution(mesh):
    spec = P("lon", "lat")
    return jax.shard_map(
        per_device, mesh=mesh, in_specs=(spec,) * 5, out_specs=spec, check_vma=False
    )
```

```python
import functools

import jax
import jax.numpy as jnp
from jax import lax
from jax.experimental import pallas as pl
from jax.experimental.pallas import tpu as pltpu
from jax.sharding import PartitionSpec as P

SUB = 8
LANE = 128
SENT = 24
BACK = 8
GROUP = 4
PARTS = 2
LEVELS = 3
F32 = jnp.float32


def unpack(piece):
    return piece[0:2], piece[2:6], piece[6:10], piece[10:12], piece[12:16], piece[16:20]


def mat_vec(m, v):
    return (m[0] * v[0] + m[1] * v[1], m[2] * v[0] + m[3] * v[1])


def mat_mat(m, k):
    return (
        m[0] * k[0] + m[1] * k[2],
        m[0] * k[1] + m[1] * k[3],
        m[2] * k[0] + m[3] * k[2],
        m[2] * k[1] + m[3] * k[3],
    )


def plus(a, b):
    return tuple(x + y for x, y in zip(a, b))


def inverse(m):
    scale = 1.0 / (m[0] * m[3] - m[1] * m[2])
    return (m[3] * scale, -(m[1] * scale), -(m[2] * scale), m[0] * scale)


def interface(west, east, constant_only=False):
    _, _, _, lc, le, lw = unpack(west)
    fc, fe, fw, _, _, _ = unpack(east)
    loop = mat_mat(fw, le)
    inv = inverse((1.0 - loop[0], -loop[1], -loop[2], 1.0 - loop[3]))
    first_c = mat_vec(inv, plus(fc, mat_vec(fw, lc)))
    last_c = plus(lc, mat_vec(le, first_c))
    if constant_only:
        return first_c, last_c
    first_e = mat_mat(inv, fe)
    first_w = mat_mat(inv, mat_mat(fw, lw))
    last_e = mat_mat(le, first_e)
    last_w = plus(lw, mat_mat(le, first_w))
    return first_c, first_e, first_w, last_c, last_e, last_w


def joined(west, east):
    meet = interface(west, east)
    first_c, first_e, first_w, last_c, last_e, last_w = meet
    fc, fe, fw, _, _, _ = unpack(west)
    _, _, _, lc, le, lw = unpack(east)
    piece = (
        plus(fc, mat_vec(fe, first_c))
        + mat_mat(fe, first_e)
        + plus(fw, mat_mat(fe, first_w))
        + plus(lc, mat_vec(lw, last_c))
        + plus(le, mat_mat(lw, last_e))
        + mat_mat(lw, last_w)
    )
    return piece, sum(meet, ())


def rolled(values, by):
    count = values[0].shape[0]
    return tuple(pltpu.roll(x, by % count, 0) for x in values)


def split_pairs(meet, east, west, step):
    first = plus(plus(meet[0:2], mat_vec(meet[2:6], east)), mat_vec(meet[6:10], west))
    last = plus(plus(meet[10:12], mat_vec(meet[12:16], east)), mat_vec(meet[16:20], west))
    count = first[0].shape[0]
    place = lax.broadcasted_iota(jnp.int32, first[0].shape, 0)
    lower = lax.rem(place, 2 * step) < step
    if 2 * step < count:
        east = rolled(east, step)
    moved = rolled(last, step)
    return (
        tuple(jnp.where(lower, a, b) for a, b in zip(first, east)),
        tuple(jnp.where(lower, a, b) for a, b in zip(west, moved)),
    )


def kernel(
    peers, t_hbm, l2_hbm, l1_hbm, u1_hbm, u2_hbm, z_hbm,
    t_s, l2_s, l1_s, u1_s, u2_s, z_s, p_s, q_s, g_s, wa_s, wb_s,
    piece_s, inner_s, send_s, recv_s, back_s, ret_s,
    in_sem, out_sem, send_sem, recv_sem, back_send_sem, back_recv_sem,
):
    _, length, lines = t_hbm.shape
    tiles = lines // LANE
    pitch = t_s.shape[1]
    group = min(GROUP, tiles)
    me = lax.axis_index("lon")
    others = [lax.rem(me + k, peers) for k in range(1, peers)]

    def owning(who, action):
        if tiles < peers:
            pl.when(who < tiles)(action)
        else:
            action()

    def loads(tile, part):
        pairs = ((t_hbm, t_s), (l2_hbm, l2_s), (l1_hbm, l1_s), (u1_hbm, u1_s), (u2_hbm, u2_s))
        some = pl.ds(part * (length // PARTS), length // PARTS)
        return [
            pltpu.make_async_copy(
                src.at[:, some, pl.ds(tile * LANE, LANE)],
                dst.at[pl.ds(tile * SUB, SUB), some, :],
                in_sem.at[idx, tile, part],
            )
            for idx, (src, dst) in enumerate(pairs)
        ]

    flat_rows = tiles * SUB * pitch
    t_f, l2_f, l1_f, u1_f, u2_f, z_f = (
        ref.reshape(flat_rows, LANE) for ref in (t_s, l2_s, l1_s, u1_s, u2_s, z_s)
    )

    for base in range(0, tiles, group):
        for part in range(PARTS):
            for tile in range(base, base + group):
                for copy in loads(tile, part):
                    copy.start()

    barrier = pltpu.get_barrier_semaphore()
    for peer in others:
        pl.semaphore_signal(
            barrier, inc=1, device_id={"lon": peer}, device_id_type=pl.DeviceIdType.MESH
        )

    ret_s[0] = jnp.zeros((SUB, LANE), F32)
    back_s[pl.ds(0, SUB), :] = jnp.ones((SUB, LANE), F32)
    zero = ret_s[0]
    one = back_s[pl.ds(0, SUB), :]

    def strided(tile, row):
        return pl.ds(tile * SUB * pitch + row, SUB, stride=pitch)

    def packed(tile):
        return pl.ds(tile * SUB, SUB)

    def outward(peer, source):
        return pltpu.make_async_remote_copy(
            src_ref=send_s.at[peer],
            dst_ref=recv_s.at[pl.ds(pl.multiple_of(source * SENT, SENT), SENT), :],
            send_sem=send_sem.at[peer],
            recv_sem=recv_sem.at[source],
            device_id={"lon": peer},
            device_id_type=pl.DeviceIdType.MESH,
        )

    def homeward(peer, source):
        return pltpu.make_async_remote_copy(
            src_ref=back_s.at[pl.ds(pl.multiple_of(peer * BACK, BACK), BACK), :],
            dst_ref=ret_s.at[source],
            send_sem=back_send_sem.at[peer],
            recv_sem=back_recv_sem.at[source],
            device_id={"lon": peer},
            device_id_type=pl.DeviceIdType.MESH,
        )

    def whole(tile, carry):
        piece = tuple(piece_s[tile, pl.ds(idx * SUB, SUB), :] for idx in range(20))
        for level in range(LEVELS):
            piece, meet = joined(piece, rolled(piece, -(1 << level)))
            for idx, value in enumerate(meet):
                inner_s[tile, pl.ds((level * 20 + idx) * SUB, SUB), :] = value
        for idx, value in enumerate(piece):
            send_s[tile, pl.ds(idx, 1), :] = value[0:1, :]
        return carry

    for base in range(0, tiles, group):
        members = list(range(base, base + group))

        def forward(i, state, members=members):
            new_state = []
            for tile, (p1, q1, g1, a1, b1, p2, q2, g2, a2, b2) in zip(members, state):
                here = strided(tile, i)
                l2, l1, u1, u2 = l2_f[here, :], l1_f[here, :], u1_f[here, :], u2_f[here, :]
                target = t_f[here, :]
                centre = (l2 + l1 + u1 + u2) - 1.0
                beta = l1 + l2 * p2
                scale = pl.reciprocal((centre - l2 * q2) - beta * p1, approx=True)
                p0 = (u1 + beta * q1) * scale
                q0 = u2 * scale
                far = l2 * scale
                near = beta * scale
                g0 = (far * g2 - target * scale) + near * g1
                a0 = far * a2 + near * a1
                b0 = far * b2 + near * b1
                at = packed(tile)
                p_s[i, at, :] = p0
                q_s[i, at, :] = q0
                g_s[i, at, :] = g0
                wa_s[i, at, :] = a0
                wb_s[i, at, :] = b0
                new_state.append((p0, q0, g0, a0, b0, p1, q1, g1, a1, b1))
            return tuple(new_state)

        start = (zero, zero, zero, zero, one, zero, zero, zero, one, zero)
        ends = (start,) * group
        for part in range(PARTS):
            for tile in members:
                for copy in loads(tile, part):
                    copy.wait()
            span = length // PARTS
            ends = lax.fori_loop(part * span, (part + 1) * span, forward, ends, unroll=4)

        def first_rows(i, state, members=members):
            new_state = []
            for tile, forms in zip(members, state):
                at = packed(tile)
                p, q, g = p_s[i, at, :], q_s[i, at, :], g_s[i, at, :]
                wa, wb = wa_s[i, at, :], wb_s[i, at, :]
                new_forms = []
                for c, x, y, a, b in forms:
                    new_forms.append((c + x * g, y + x * p, x * q, a + x * wa, b + x * wb))
                new_state.append(tuple(new_forms))
            return tuple(new_state)

        forms = ((zero, one, zero, zero, zero), (zero, zero, one, zero, zero))
        firsts = lax.fori_loop(0, length, first_rows, (forms,) * group, unroll=8)

        for tile, end, (f0, f1) in zip(members, ends, firsts):
            p1, q1, g1, a1, b1, p2, q2, g2, a2, b2 = end
            piece = (
                f0[0], f1[0],
                f0[1], f0[2], f1[1], f1[2],
                f0[3], f0[4], f1[3], f1[4],
                g2 + p2 * g1, g1,
                p2 * p1 + q2, p2 * q1, p1, q1,
                p2 * a1 + a2, p2 * b1 + b2, a1, b1,
            )
            for idx, value in enumerate(piece):
                piece_s[tile, pl.ds(idx * SUB, SUB), :] = value

        lax.fori_loop(base, base + group, whole, 0, unroll=2)
        if base == 0:
            pl.semaphore_wait(barrier, peers - 1)
        for tile in members:
            pl.when(me != tile)(lambda tile=tile: outward(tile, me).start())

    def solve_lines():
        recv_s[pl.ds(pl.multiple_of(me * SENT, SENT), SENT), :] = send_s[me]
        for peer in others:
            outward(me, peer).wait_recv()
        piece = tuple(recv_s[pl.ds(idx, peers, stride=SENT), :] for idx in range(20))
        meets = []
        step = 1
        while 2 * step < peers:
            piece, meet = joined(piece, rolled(piece, -step))
            meets.append(meet)
            step *= 2
        first, last = interface(piece, rolled(piece, -step), True)
        place = lax.broadcasted_iota(jnp.int32, (peers, LANE), 0)
        east = tuple(jnp.where(place < step, x, 0.0) for x in first)
        west = tuple(jnp.where(place < step, 0.0, x) for x in rolled(last, step))
        for meet in reversed(meets):
            step //= 2
            east, west = split_pairs(meet, east, west, step)
        for idx, value in enumerate(east + west):
            back_s[pl.ds(idx, peers, stride=BACK), :] = value
        for peer in others:
            homeward(peer, me).start()
        ret_s[me] = back_s[pl.ds(pl.multiple_of(me * BACK, BACK), BACK), :]

    owning(me, solve_lines)

    def store(tile, part):
        some = pl.ds(part * (length // PARTS), length // PARTS)
        return pltpu.make_async_copy(
            z_s.at[pl.ds(tile * SUB, SUB), some, :],
            z_hbm.at[:, some, pl.ds(tile * LANE, LANE)],
            out_sem.at[tile, part],
        )

    for base in range(0, tiles, group):
        members = list(range(base, base + group))
        start, bounds = [], []
        for tile in members:
            pl.when(me != tile)(lambda tile=tile: homeward(me, tile).wait_recv())
        for tile in members:
            e0, e1, w0, w1 = (
                jnp.broadcast_to(ret_s[tile, pl.ds(idx, 1), :], (SUB, LANE)) for idx in range(4)
            )
            east, west = (e0, e1), (w0, w1)
            for level in reversed(range(LEVELS)):
                meet = tuple(
                    inner_s[tile, pl.ds((level * 20 + idx) * SUB, SUB), :] for idx in range(20)
                )
                east, west = split_pairs(meet, east, west, 1 << level)
            start.append(east)
            bounds.append(west)

        def backward(step, state, members=members, bounds=bounds):
            i = length - 1 - step
            new_state = []
            for tile, (wa, wb), (x1, x2) in zip(members, bounds, state):
                at = packed(tile)
                free = (g_s[i, at, :] + wa_s[i, at, :] * wa) + wb_s[i, at, :] * wb
                x0 = (free + q_s[i, at, :] * x2) + p_s[i, at, :] * x1
                z_f[strided(tile, i), :] = 2.0 * x0 - t_f[strided(tile, i), :]
                new_state.append((x0, x1))
            return tuple(new_state)

        state = tuple(start)
        for part in reversed(range(PARTS)):
            span = length // PARTS
            done = (PARTS - 1 - part) * span
            state = lax.fori_loop(done, done + span, backward, state, unroll=8)
            for tile in members:
                store(tile, part).start()

    for tile in range(tiles):
        for part in range(PARTS):
            store(tile, part).wait()
    for tile in range(tiles):
        pl.when(me != tile)(lambda tile=tile: outward(tile, me).wait_send())

    def sent_home():
        for peer in others:
            homeward(peer, me).wait_send()

    owning(me, sent_home)


def per_device(tracer, lower2, lower1, upper1, upper2):
    rows, lines = tracer.shape
    peers = lax.axis_size("lon")
    tiles = lines // LANE
    assert rows % (PARTS * SUB * SUB) == 0 and peers & (peers - 1) == 0 and lines % LANE == 0 and tiles <= peers
    assert tiles % min(GROUP, tiles) == 0
    length = rows // SUB
    pitch = length if length % (2 * SUB) else length + SUB
    plane = pltpu.VMEM((tiles * SUB, pitch, LANE), F32)
    factor = pltpu.VMEM((length, tiles * SUB, LANE), F32)
    sem = pltpu.SemaphoreType.DMA
    solved = pl.pallas_call(
        functools.partial(kernel, peers),
        out_shape=jax.ShapeDtypeStruct((SUB, length, lines), F32),
        in_specs=[pl.BlockSpec(memory_space=pl.ANY)] * 5,
        out_specs=pl.BlockSpec(memory_space=pl.ANY),
        scratch_shapes=[plane] * 6
        + [factor] * 5
        + [
            pltpu.VMEM((tiles, 20 * SUB, LANE), F32),
            pltpu.VMEM((tiles, LEVELS * 20 * SUB, LANE), F32),
            pltpu.VMEM((tiles, SENT, LANE), F32),
            pltpu.VMEM((peers * SENT, LANE), F32),
            pltpu.VMEM((peers * BACK, LANE), F32),
            pltpu.VMEM((tiles, BACK, LANE), F32),
            sem((5, tiles, PARTS)),
            sem((tiles, PARTS)),
            sem((peers,)),
            sem((peers,)),
            sem((peers,)),
            sem((peers,)),
        ],
        compiler_params=pltpu.CompilerParams(
            collective_id=0, has_side_effects=True, vmem_limit_bytes=50 * 1024 * 1024
        ),
        cost_estimate=pl.CostEstimate(
            flops=90 * rows * lines, bytes_accessed=24 * rows * lines, transcendentals=0
        ),
    )(*(x.reshape(SUB, length, lines) for x in (tracer, lower2, lower1, upper1, upper2)))
    return solved.reshape(rows, lines)


def solution(mesh):
    spec = P("lon", "lat")
    return jax.shard_map(
        per_device, mesh=mesh, in_specs=(spec,) * 5, out_specs=spec, check_vma=False
    )
```

```python
import functools

import jax
import jax.numpy as jnp
from jax import lax
from jax.experimental import pallas as pl
from jax.experimental.pallas import tpu as pltpu
from jax.sharding import PartitionSpec as P

SUB = 8
LANE = 128
SENT = 24
BACK = 8
GROUP = 4
PARTS = 2
LEVELS = 3
F32 = jnp.float32


def unpack(piece):
    return piece[0:2], piece[2:6], piece[6:10], piece[10:12], piece[12:16], piece[16:20]


def mat_vec(m, v):
    return (m[0] * v[0] + m[1] * v[1], m[2] * v[0] + m[3] * v[1])


def mat_mat(m, k):
    return (
        m[0] * k[0] + m[1] * k[2],
        m[0] * k[1] + m[1] * k[3],
        m[2] * k[0] + m[3] * k[2],
        m[2] * k[1] + m[3] * k[3],
    )


def plus(a, b):
    return tuple(x + y for x, y in zip(a, b))


def inverse(m):
    scale = 1.0 / (m[0] * m[3] - m[1] * m[2])
    return (m[3] * scale, -(m[1] * scale), -(m[2] * scale), m[0] * scale)


def interface(west, east, constant_only=False):
    _, _, _, lc, le, lw = unpack(west)
    fc, fe, fw, _, _, _ = unpack(east)
    loop = mat_mat(fw, le)
    inv = inverse((1.0 - loop[0], -loop[1], -loop[2], 1.0 - loop[3]))
    first_c = mat_vec(inv, plus(fc, mat_vec(fw, lc)))
    last_c = plus(lc, mat_vec(le, first_c))
    if constant_only:
        return first_c, last_c
    first_e = mat_mat(inv, fe)
    first_w = mat_mat(inv, mat_mat(fw, lw))
    last_e = mat_mat(le, first_e)
    last_w = plus(lw, mat_mat(le, first_w))
    return first_c, first_e, first_w, last_c, last_e, last_w


def joined(west, east):
    meet = interface(west, east)
    first_c, first_e, first_w, last_c, last_e, last_w = meet
    fc, fe, fw, _, _, _ = unpack(west)
    _, _, _, lc, le, lw = unpack(east)
    piece = (
        plus(fc, mat_vec(fe, first_c))
        + mat_mat(fe, first_e)
        + plus(fw, mat_mat(fe, first_w))
        + plus(lc, mat_vec(lw, last_c))
        + plus(le, mat_mat(lw, last_e))
        + mat_mat(lw, last_w)
    )
    return piece, sum(meet, ())


def rolled(values, by):
    count = values[0].shape[0]
    return tuple(pltpu.roll(x, by % count, 0) for x in values)


def split_pairs(meet, east, west, step):
    first = plus(plus(meet[0:2], mat_vec(meet[2:6], east)), mat_vec(meet[6:10], west))
    last = plus(plus(meet[10:12], mat_vec(meet[12:16], east)), mat_vec(meet[16:20], west))
    count = first[0].shape[0]
    place = lax.broadcasted_iota(jnp.int32, first[0].shape, 0)
    lower = lax.rem(place, 2 * step) < step
    if 2 * step < count:
        east = rolled(east, step)
    moved = rolled(last, step)
    return (
        tuple(jnp.where(lower, a, b) for a, b in zip(first, east)),
        tuple(jnp.where(lower, a, b) for a, b in zip(west, moved)),
    )


def kernel(
    peers, t_hbm, l2_hbm, l1_hbm, u1_hbm, u2_hbm, z_hbm,
    t_s, l2_s, l1_s, u1_s, u2_s, z_s, p_s, q_s, g_s, wa_s, wb_s,
    piece_s, inner_s, send_s, recv_s, back_s, ret_s,
    in_sem, out_sem, send_sem, recv_sem, back_send_sem, back_recv_sem,
):
    _, length, lines = t_hbm.shape
    tiles = lines // LANE
    pitch = t_s.shape[1]
    group = min(GROUP, tiles)
    me = lax.axis_index("lon")
    others = [lax.rem(me + k, peers) for k in range(1, peers)]

    def owning(who, action):
        if tiles < peers:
            pl.when(who < tiles)(action)
        else:
            action()

    def loads(tile, part):
        pairs = ((t_hbm, t_s), (l2_hbm, l2_s), (l1_hbm, l1_s), (u1_hbm, u1_s), (u2_hbm, u2_s))
        some = pl.ds(part * (length // PARTS), length // PARTS)
        return [
            pltpu.make_async_copy(
                src.at[:, some, pl.ds(tile * LANE, LANE)],
                dst.at[pl.ds(tile * SUB, SUB), some, :],
                in_sem.at[idx, tile, part],
            )
            for idx, (src, dst) in enumerate(pairs)
        ]

    flat_rows = (tiles + 1) * SUB * pitch
    t_f, l2_f, l1_f, u1_f, u2_f, z_f = (
        ref.reshape(flat_rows, LANE) for ref in (t_s, l2_s, l1_s, u1_s, u2_s, z_s)
    )

    def start_loads(base):
        for part in range(PARTS):
            for tile in range(base, base + group):
                for copy in loads(tile, part):
                    copy.start()

    start_loads(0)

    barrier = pltpu.get_barrier_semaphore()
    for peer in others:
        pl.semaphore_signal(
            barrier, inc=1, device_id={"lon": peer}, device_id_type=pl.DeviceIdType.MESH
        )

    ret_s[0] = jnp.zeros((SUB, LANE), F32)
    back_s[pl.ds(0, SUB), :] = jnp.ones((SUB, LANE), F32)
    zero = ret_s[0]
    one = back_s[pl.ds(0, SUB), :]

    def strided(tile, row):
        return pl.ds(tile * SUB * pitch + row, SUB, stride=pitch)

    def packed(tile):
        return pl.ds(tile * SUB, SUB)

    def outward(peer, source):
        return pltpu.make_async_remote_copy(
            src_ref=send_s.at[peer],
            dst_ref=recv_s.at[pl.ds(pl.multiple_of(source * SENT, SENT), SENT), :],
            send_sem=send_sem.at[peer],
            recv_sem=recv_sem.at[source],
            device_id={"lon": peer},
            device_id_type=pl.DeviceIdType.MESH,
        )

    def homeward(peer, source):
        return pltpu.make_async_remote_copy(
            src_ref=back_s.at[pl.ds(pl.multiple_of(peer * BACK, BACK), BACK), :],
            dst_ref=ret_s.at[source],
            send_sem=back_send_sem.at[peer],
            recv_sem=back_recv_sem.at[source],
            device_id={"lon": peer},
            device_id_type=pl.DeviceIdType.MESH,
        )

    def whole(tile, carry):
        piece = tuple(piece_s[tile, pl.ds(idx * SUB, SUB), :] for idx in range(20))
        for level in range(LEVELS):
            piece, meet = joined(piece, rolled(piece, -(1 << level)))
            for idx, value in enumerate(meet):
                inner_s[tile, pl.ds((level * 20 + idx) * SUB, SUB), :] = value
        for idx, value in enumerate(piece):
            send_s[tile, pl.ds(idx, 1), :] = value[0:1, :]
        return carry

    for base in range(0, tiles, group):
        members = list(range(base, base + group))

        def forward(i, state, members=members):
            new_state = []
            for tile, (p1, q1, g1, a1, b1, p2, q2, g2, a2, b2) in zip(members, state):
                here = strided(tile, i)
                l2, l1, u1, u2 = l2_f[here, :], l1_f[here, :], u1_f[here, :], u2_f[here, :]
                target = t_f[here, :]
                centre = (l2 + l1 + u1 + u2) - 1.0
                beta = l1 + l2 * p2
                scale = pl.reciprocal((centre - l2 * q2) - beta * p1, approx=True)
                p0 = (u1 + beta * q1) * scale
                q0 = u2 * scale
                far = l2 * scale
                near = beta * scale
                g0 = (far * g2 - target * scale) + near * g1
                a0 = far * a2 + near * a1
                b0 = far * b2 + near * b1
                at = packed(tile)
                p_s[i, at, :] = p0
                q_s[i, at, :] = q0
                g_s[i, at, :] = g0
                wa_s[i, at, :] = a0
                wb_s[i, at, :] = b0
                new_state.append((p0, q0, g0, a0, b0, p1, q1, g1, a1, b1))
            return tuple(new_state)

        start = (zero, zero, zero, zero, one, zero, zero, zero, one, zero)
        ends = (start,) * group
        for part in range(PARTS):
            for tile in members:
                for copy in loads(tile, part):
                    copy.wait()
            span = length // PARTS
            ends = lax.fori_loop(part * span, (part + 1) * span, forward, ends, unroll=4)
            if part == 0 and base + group < tiles:
                start_loads(base + group)

        def first_rows(i, state, members=members):
            new_state = []
            for tile, forms in zip(members, state):
                at = packed(tile)
                p, q, g = p_s[i, at, :], q_s[i, at, :], g_s[i, at, :]
                wa, wb = wa_s[i, at, :], wb_s[i, at, :]
                new_forms = []
                for c, x, y, a, b in forms:
                    new_forms.append((c + x * g, y + x * p, x * q, a + x * wa, b + x * wb))
                new_state.append(tuple(new_forms))
            return tuple(new_state)

        forms = ((zero, one, zero, zero, zero), (zero, zero, one, zero, zero))
        firsts = lax.fori_loop(0, length, first_rows, (forms,) * group, unroll=8)

        for tile, end, (f0, f1) in zip(members, ends, firsts):
            p1, q1, g1, a1, b1, p2, q2, g2, a2, b2 = end
            piece = (
                f0[0], f1[0],
                f0[1], f0[2], f1[1], f1[2],
                f0[3], f0[4], f1[3], f1[4],
                g2 + p2 * g1, g1,
                p2 * p1 + q2, p2 * q1, p1, q1,
                p2 * a1 + a2, p2 * b1 + b2, a1, b1,
            )
            for idx, value in enumerate(piece):
                piece_s[tile, pl.ds(idx * SUB, SUB), :] = value

        lax.fori_loop(base, base + group, whole, 0, unroll=2)
        if base == 0:
            pl.semaphore_wait(barrier, peers - 1)
        for tile in members:
            pl.when(me != tile)(lambda tile=tile: outward(tile, me).start())

    def solve_lines():
        recv_s[pl.ds(pl.multiple_of(me * SENT, SENT), SENT), :] = send_s[me]
        for peer in others:
            outward(me, peer).wait_recv()
        piece = tuple(recv_s[pl.ds(idx, peers, stride=SENT), :] for idx in range(20))
        meets = []
        step = 1
        while 2 * step < peers:
            piece, meet = joined(piece, rolled(piece, -step))
            meets.append(meet)
            step *= 2
        first, last = interface(piece, rolled(piece, -step), True)
        place = lax.broadcasted_iota(jnp.int32, (peers, LANE), 0)
        east = tuple(jnp.where(place < step, x, 0.0) for x in first)
        west = tuple(jnp.where(place < step, 0.0, x) for x in rolled(last, step))
        for meet in reversed(meets):
            step //= 2
            east, west = split_pairs(meet, east, west, step)
        for idx, value in enumerate(east + west):
            back_s[pl.ds(idx, peers, stride=BACK), :] = value
        for peer in others:
            homeward(peer, me).start()
        ret_s[me] = back_s[pl.ds(pl.multiple_of(me * BACK, BACK), BACK), :]

    owning(me, solve_lines)

    def store(tile, part):
        some = pl.ds(part * (length // PARTS), length // PARTS)
        return pltpu.make_async_copy(
            z_s.at[pl.ds(tile * SUB, SUB), some, :],
            z_hbm.at[:, some, pl.ds(tile * LANE, LANE)],
            out_sem.at[tile, part],
        )

    for base in range(0, tiles, group):
        members = list(range(base, base + group))
        start, bounds = [], []
        for tile in members:
            pl.when(me != tile)(lambda tile=tile: homeward(me, tile).wait_recv())
        for tile in members:
            e0, e1, w0, w1 = (
                jnp.broadcast_to(ret_s[tile, pl.ds(idx, 1), :], (SUB, LANE)) for idx in range(4)
            )
            east, west = (e0, e1), (w0, w1)
            for level in reversed(range(LEVELS)):
                meet = tuple(
                    inner_s[tile, pl.ds((level * 20 + idx) * SUB, SUB), :] for idx in range(20)
                )
                east, west = split_pairs(meet, east, west, 1 << level)
            start.append(east)
            bounds.append(west)

        def backward(step, state, members=members, bounds=bounds):
            i = length - 1 - step
            new_state = []
            for tile, (wa, wb), (x1, x2) in zip(members, bounds, state):
                at = packed(tile)
                free = (g_s[i, at, :] + wa_s[i, at, :] * wa) + wb_s[i, at, :] * wb
                x0 = (free + q_s[i, at, :] * x2) + p_s[i, at, :] * x1
                z_f[strided(tile, i), :] = 2.0 * x0 - t_f[strided(tile, i), :]
                new_state.append((x0, x1))
            return tuple(new_state)

        state = tuple(start)
        for part in reversed(range(PARTS)):
            span = length // PARTS
            done = (PARTS - 1 - part) * span
            state = lax.fori_loop(done, done + span, backward, state, unroll=8)
            for tile in members:
                store(tile, part).start()

    for tile in range(tiles):
        for part in range(PARTS):
            store(tile, part).wait()
    for tile in range(tiles):
        pl.when(me != tile)(lambda tile=tile: outward(tile, me).wait_send())

    def sent_home():
        for peer in others:
            homeward(peer, me).wait_send()

    owning(me, sent_home)


def per_device(tracer, lower2, lower1, upper1, upper2):
    rows, lines = tracer.shape
    peers = lax.axis_size("lon")
    tiles = lines // LANE
    assert rows % (PARTS * SUB * SUB) == 0 and peers & (peers - 1) == 0 and lines % LANE == 0 and tiles <= peers
    assert tiles % min(GROUP, tiles) == 0
    length = rows // SUB
    pitch = length if length % (2 * SUB) else length + SUB
    plane = pltpu.VMEM(((tiles + 1) * SUB, pitch, LANE), F32)
    factor = pltpu.VMEM((length, tiles * SUB, LANE), F32)
    sem = pltpu.SemaphoreType.DMA
    solved = pl.pallas_call(
        functools.partial(kernel, peers),
        out_shape=jax.ShapeDtypeStruct((SUB, length, lines), F32),
        in_specs=[pl.BlockSpec(memory_space=pl.ANY)] * 5,
        out_specs=pl.BlockSpec(memory_space=pl.ANY),
        scratch_shapes=[plane] * 6
        + [factor] * 5
        + [
            pltpu.VMEM((tiles, 20 * SUB, LANE), F32),
            pltpu.VMEM((tiles, LEVELS * 20 * SUB, LANE), F32),
            pltpu.VMEM((tiles, SENT, LANE), F32),
            pltpu.VMEM(((peers + 1) * SENT, LANE), F32),
            pltpu.VMEM(((peers + 1) * BACK, LANE), F32),
            pltpu.VMEM((tiles, BACK, LANE), F32),
            sem((5, tiles, PARTS)),
            sem((tiles, PARTS)),
            sem((peers,)),
            sem((peers,)),
            sem((peers,)),
            sem((peers,)),
        ],
        compiler_params=pltpu.CompilerParams(
            collective_id=0, has_side_effects=True, vmem_limit_bytes=50 * 1024 * 1024
        ),
        cost_estimate=pl.CostEstimate(
            flops=90 * rows * lines, bytes_accessed=24 * rows * lines, transcendentals=0
        ),
    )(*(x.reshape(SUB, length, lines) for x in (tracer, lower2, lower1, upper1, upper2)))
    return solved.reshape(rows, lines)


def solution(mesh):
    spec = P("lon", "lat")
    return jax.shard_map(
        per_device, mesh=mesh, in_specs=(spec,) * 5, out_specs=spec, check_vma=False
    )
```

```python
import functools

import jax
import jax.numpy as jnp
from jax import lax
from jax.experimental import pallas as pl
from jax.experimental.pallas import tpu as pltpu
from jax.sharding import PartitionSpec as P

SUB = 8
LANE = 128
SENT = 24
BACK = 8
GROUP = 4
PARTS = 2
LEVELS = 3
F32 = jnp.float32


def unpack(piece):
    return piece[0:2], piece[2:6], piece[6:10], piece[10:12], piece[12:16], piece[16:20]


def mat_vec(m, v):
    return (m[0] * v[0] + m[1] * v[1], m[2] * v[0] + m[3] * v[1])


def mat_mat(m, k):
    return (
        m[0] * k[0] + m[1] * k[2],
        m[0] * k[1] + m[1] * k[3],
        m[2] * k[0] + m[3] * k[2],
        m[2] * k[1] + m[3] * k[3],
    )


def plus(a, b):
    return tuple(x + y for x, y in zip(a, b))


def inverse(m):
    scale = 1.0 / (m[0] * m[3] - m[1] * m[2])
    return (m[3] * scale, -(m[1] * scale), -(m[2] * scale), m[0] * scale)


def interface(west, east, constant_only=False):
    _, _, _, lc, le, lw = unpack(west)
    fc, fe, fw, _, _, _ = unpack(east)
    loop = mat_mat(fw, le)
    inv = inverse((1.0 - loop[0], -loop[1], -loop[2], 1.0 - loop[3]))
    first_c = mat_vec(inv, plus(fc, mat_vec(fw, lc)))
    last_c = plus(lc, mat_vec(le, first_c))
    if constant_only:
        return first_c, last_c
    first_e = mat_mat(inv, fe)
    first_w = mat_mat(inv, mat_mat(fw, lw))
    last_e = mat_mat(le, first_e)
    last_w = plus(lw, mat_mat(le, first_w))
    return first_c, first_e, first_w, last_c, last_e, last_w


def joined(west, east):
    meet = interface(west, east)
    first_c, first_e, first_w, last_c, last_e, last_w = meet
    fc, fe, fw, _, _, _ = unpack(west)
    _, _, _, lc, le, lw = unpack(east)
    piece = (
        plus(fc, mat_vec(fe, first_c))
        + mat_mat(fe, first_e)
        + plus(fw, mat_mat(fe, first_w))
        + plus(lc, mat_vec(lw, last_c))
        + plus(le, mat_mat(lw, last_e))
        + mat_mat(lw, last_w)
    )
    return piece, sum(meet, ())


def rolled(values, by):
    count = values[0].shape[0]
    return tuple(pltpu.roll(x, by % count, 0) for x in values)


def split_pairs(meet, east, west, step):
    first = plus(plus(meet[0:2], mat_vec(meet[2:6], east)), mat_vec(meet[6:10], west))
    last = plus(plus(meet[10:12], mat_vec(meet[12:16], east)), mat_vec(meet[16:20], west))
    count = first[0].shape[0]
    place = lax.broadcasted_iota(jnp.int32, first[0].shape, 0)
    lower = lax.rem(place, 2 * step) < step
    if 2 * step < count:
        east = rolled(east, step)
    moved = rolled(last, step)
    return (
        tuple(jnp.where(lower, a, b) for a, b in zip(first, east)),
        tuple(jnp.where(lower, a, b) for a, b in zip(west, moved)),
    )


def kernel(
    peers, t_hbm, l2_hbm, l1_hbm, u1_hbm, u2_hbm, z_hbm,
    t_s, l2_s, l1_s, u1_s, u2_s, z_s, p_s, q_s, g_s, wa_s, wb_s,
    piece_s, inner_s, send_s, recv_s, back_s, ret_s,
    in_sem, out_sem, send_sem, recv_sem, back_send_sem, back_recv_sem,
):
    _, length, lines = t_hbm.shape
    tiles = lines // LANE
    pitch = t_s.shape[1]
    group = min(GROUP, tiles)
    me = lax.axis_index("lon")
    others = [lax.rem(me + k, peers) for k in range(1, peers)]

    def owning(who, action):
        if tiles < peers:
            pl.when(who < tiles)(action)
        else:
            action()

    def loads(tile, part):
        pairs = ((t_hbm, t_s), (l2_hbm, l2_s), (l1_hbm, l1_s), (u1_hbm, u1_s), (u2_hbm, u2_s))
        some = pl.ds(part * (length // PARTS), length // PARTS)
        return [
            pltpu.make_async_copy(
                src.at[:, some, pl.ds(tile * LANE, LANE)],
                dst.at[pl.ds(tile * SUB, SUB), some, :],
                in_sem.at[idx, tile, part],
            )
            for idx, (src, dst) in enumerate(pairs)
        ]

    flat_rows = (tiles + 1) * SUB * pitch
    t_f, l2_f, l1_f, u1_f, u2_f, z_f = (
        ref.reshape(flat_rows, LANE) for ref in (t_s, l2_s, l1_s, u1_s, u2_s, z_s)
    )

    def start_loads(base):
        for part in range(PARTS):
            for tile in range(base, base + group):
                for copy in loads(tile, part):
                    copy.start()

    start_loads(0)

    barrier = pltpu.get_barrier_semaphore()
    for peer in others:
        pl.semaphore_signal(
            barrier, inc=1, device_id={"lon": peer}, device_id_type=pl.DeviceIdType.MESH
        )

    ret_s[0] = jnp.zeros((SUB, LANE), F32)
    back_s[pl.ds(0, SUB), :] = jnp.ones((SUB, LANE), F32)
    zero = ret_s[0]
    one = back_s[pl.ds(0, SUB), :]

    def strided(tile, row):
        return pl.ds(tile * SUB * pitch + row, SUB, stride=pitch)

    def packed(tile):
        return pl.ds(tile * SUB, SUB)

    def outward(peer, source):
        return pltpu.make_async_remote_copy(
            src_ref=send_s.at[peer],
            dst_ref=recv_s.at[pl.ds(pl.multiple_of(source * SENT, SENT), SENT), :],
            send_sem=send_sem.at[peer],
            recv_sem=recv_sem.at[source],
            device_id={"lon": peer},
            device_id_type=pl.DeviceIdType.MESH,
        )

    def homeward(peer, source):
        return pltpu.make_async_remote_copy(
            src_ref=back_s.at[pl.ds(pl.multiple_of(peer * BACK, BACK), BACK), :],
            dst_ref=ret_s.at[source],
            send_sem=back_send_sem.at[peer],
            recv_sem=back_recv_sem.at[source],
            device_id={"lon": peer},
            device_id_type=pl.DeviceIdType.MESH,
        )

    def whole(tile, carry):
        piece = tuple(piece_s[tile, pl.ds(idx * SUB, SUB), :] for idx in range(20))
        for level in range(LEVELS):
            piece, meet = joined(piece, rolled(piece, -(1 << level)))
            for idx, value in enumerate(meet):
                inner_s[tile, pl.ds((level * 20 + idx) * SUB, SUB), :] = value
        for idx, value in enumerate(piece):
            send_s[tile, pl.ds(idx, 1), :] = value[0:1, :]
        return carry

    for base in range(0, tiles, group):
        members = list(range(base, base + group))

        def forward(i, state, members=members):
            new_state = []
            for tile, (rows_state, forms) in zip(members, state):
                p1, q1, g1, a1, b1, p2, q2, g2, a2, b2 = rows_state
                here = strided(tile, i)
                l2, l1, u1, u2 = l2_f[here, :], l1_f[here, :], u1_f[here, :], u2_f[here, :]
                target = t_f[here, :]
                centre = (l2 + l1 + u1 + u2) - 1.0
                beta = l1 + l2 * p2
                scale = pl.reciprocal((centre - l2 * q2) - beta * p1, approx=True)
                p0 = (u1 + beta * q1) * scale
                q0 = u2 * scale
                far = l2 * scale
                near = beta * scale
                g0 = (far * g2 - target * scale) + near * g1
                a0 = far * a2 + near * a1
                b0 = far * b2 + near * b1
                at = packed(tile)
                p_s[i, at, :] = p0
                q_s[i, at, :] = q0
                g_s[i, at, :] = g0
                wa_s[i, at, :] = a0
                wb_s[i, at, :] = b0
                new_forms = tuple(
                    (c + x * g0, y + x * p0, x * q0, a + x * a0, b + x * b0)
                    for c, x, y, a, b in forms
                )
                new_state.append(((p0, q0, g0, a0, b0, p1, q1, g1, a1, b1), new_forms))
            return tuple(new_state)

        start = (zero, zero, zero, zero, one, zero, zero, zero, one, zero)
        forms = ((zero, one, zero, zero, zero), (zero, zero, one, zero, zero))
        ends = ((start, forms),) * group
        for part in range(PARTS):
            for tile in members:
                for copy in loads(tile, part):
                    copy.wait()
            span = length // PARTS
            ends = lax.fori_loop(part * span, (part + 1) * span, forward, ends, unroll=4)
            if part == 0 and base + group < tiles:
                start_loads(base + group)

        for tile, (end, (f0, f1)) in zip(members, ends):
            p1, q1, g1, a1, b1, p2, q2, g2, a2, b2 = end
            piece = (
                f0[0], f1[0],
                f0[1], f0[2], f1[1], f1[2],
                f0[3], f0[4], f1[3], f1[4],
                g2 + p2 * g1, g1,
                p2 * p1 + q2, p2 * q1, p1, q1,
                p2 * a1 + a2, p2 * b1 + b2, a1, b1,
            )
            for idx, value in enumerate(piece):
                piece_s[tile, pl.ds(idx * SUB, SUB), :] = value

        lax.fori_loop(base, base + group, whole, 0, unroll=2)
        if base == 0:
            pl.semaphore_wait(barrier, peers - 1)
        for tile in members:
            pl.when(me != tile)(lambda tile=tile: outward(tile, me).start())

    def solve_lines():
        recv_s[pl.ds(pl.multiple_of(me * SENT, SENT), SENT), :] = send_s[me]
        for peer in others:
            outward(me, peer).wait_recv()
        piece = tuple(recv_s[pl.ds(idx, peers, stride=SENT), :] for idx in range(20))
        meets = []
        step = 1
        while 2 * step < peers:
            piece, meet = joined(piece, rolled(piece, -step))
            meets.append(meet)
            step *= 2
        first, last = interface(piece, rolled(piece, -step), True)
        place = lax.broadcasted_iota(jnp.int32, (peers, LANE), 0)
        east = tuple(jnp.where(place < step, x, 0.0) for x in first)
        west = tuple(jnp.where(place < step, 0.0, x) for x in rolled(last, step))
        for meet in reversed(meets):
            step //= 2
            east, west = split_pairs(meet, east, west, step)
        for idx, value in enumerate(east + west):
            back_s[pl.ds(idx, peers, stride=BACK), :] = value
        for peer in others:
            homeward(peer, me).start()
        ret_s[me] = back_s[pl.ds(pl.multiple_of(me * BACK, BACK), BACK), :]

    owning(me, solve_lines)

    def store(tile, part):
        some = pl.ds(part * (length // PARTS), length // PARTS)
        return pltpu.make_async_copy(
            z_s.at[pl.ds(tile * SUB, SUB), some, :],
            z_hbm.at[:, some, pl.ds(tile * LANE, LANE)],
            out_sem.at[tile, part],
        )

    for base in range(0, tiles, group):
        members = list(range(base, base + group))
        start, bounds = [], []
        for tile in members:
            pl.when(me != tile)(lambda tile=tile: homeward(me, tile).wait_recv())
        for tile in members:
            e0, e1, w0, w1 = (
                jnp.broadcast_to(ret_s[tile, pl.ds(idx, 1), :], (SUB, LANE)) for idx in range(4)
            )
            east, west = (e0, e1), (w0, w1)
            for level in reversed(range(LEVELS)):
                meet = tuple(
                    inner_s[tile, pl.ds((level * 20 + idx) * SUB, SUB), :] for idx in range(20)
                )
                east, west = split_pairs(meet, east, west, 1 << level)
            start.append(east)
            bounds.append(west)

        def backward(step, state, members=members, bounds=bounds):
            i = length - 1 - step
            new_state = []
            for tile, (wa, wb), (x1, x2) in zip(members, bounds, state):
                at = packed(tile)
                free = (g_s[i, at, :] + wa_s[i, at, :] * wa) + wb_s[i, at, :] * wb
                x0 = (free + q_s[i, at, :] * x2) + p_s[i, at, :] * x1
                z_f[strided(tile, i), :] = 2.0 * x0 - t_f[strided(tile, i), :]
                new_state.append((x0, x1))
            return tuple(new_state)

        state = tuple(start)
        for part in reversed(range(PARTS)):
            span = length // PARTS
            done = (PARTS - 1 - part) * span
            state = lax.fori_loop(done, done + span, backward, state, unroll=8)
            for tile in members:
                store(tile, part).start()

    for tile in range(tiles):
        for part in range(PARTS):
            store(tile, part).wait()
    for tile in range(tiles):
        pl.when(me != tile)(lambda tile=tile: outward(tile, me).wait_send())

    def sent_home():
        for peer in others:
            homeward(peer, me).wait_send()

    owning(me, sent_home)


def per_device(tracer, lower2, lower1, upper1, upper2):
    rows, lines = tracer.shape
    peers = lax.axis_size("lon")
    tiles = lines // LANE
    assert rows % (PARTS * SUB * SUB) == 0 and peers & (peers - 1) == 0 and lines % LANE == 0 and tiles <= peers
    assert tiles % min(GROUP, tiles) == 0
    length = rows // SUB
    pitch = length if length % (2 * SUB) else length + SUB
    plane = pltpu.VMEM(((tiles + 1) * SUB, pitch, LANE), F32)
    factor = pltpu.VMEM((length, tiles * SUB, LANE), F32)
    sem = pltpu.SemaphoreType.DMA
    solved = pl.pallas_call(
        functools.partial(kernel, peers),
        out_shape=jax.ShapeDtypeStruct((SUB, length, lines), F32),
        in_specs=[pl.BlockSpec(memory_space=pl.ANY)] * 5,
        out_specs=pl.BlockSpec(memory_space=pl.ANY),
        scratch_shapes=[plane] * 6
        + [factor] * 5
        + [
            pltpu.VMEM((tiles, 20 * SUB, LANE), F32),
            pltpu.VMEM((tiles, LEVELS * 20 * SUB, LANE), F32),
            pltpu.VMEM((tiles, SENT, LANE), F32),
            pltpu.VMEM(((peers + 1) * SENT, LANE), F32),
            pltpu.VMEM(((peers + 1) * BACK, LANE), F32),
            pltpu.VMEM((tiles, BACK, LANE), F32),
            sem((5, tiles, PARTS)),
            sem((tiles, PARTS)),
            sem((peers,)),
            sem((peers,)),
            sem((peers,)),
            sem((peers,)),
        ],
        compiler_params=pltpu.CompilerParams(
            collective_id=0, has_side_effects=True, vmem_limit_bytes=50 * 1024 * 1024
        ),
        cost_estimate=pl.CostEstimate(
            flops=90 * rows * lines, bytes_accessed=24 * rows * lines, transcendentals=0
        ),
    )(*(x.reshape(SUB, length, lines) for x in (tracer, lower2, lower1, upper1, upper2)))
    return solved.reshape(rows, lines)


def solution(mesh):
    spec = P("lon", "lat")
    return jax.shard_map(
        per_device, mesh=mesh, in_specs=(spec,) * 5, out_specs=spec, check_vma=False
    )
```

```python
import functools

import jax
import jax.numpy as jnp
from jax import lax
from jax.experimental import pallas as pl
from jax.experimental.pallas import tpu as pltpu
from jax.sharding import PartitionSpec as P

SUB = 8
LANE = 128
SENT = 24
BACK = 8
GROUP = 4
PARTS = 2
LEVELS = 3
F32 = jnp.float32


def unpack(piece):
    return piece[0:2], piece[2:6], piece[6:10], piece[10:12], piece[12:16], piece[16:20]


def mat_vec(m, v):
    return (m[0] * v[0] + m[1] * v[1], m[2] * v[0] + m[3] * v[1])


def mat_mat(m, k):
    return (
        m[0] * k[0] + m[1] * k[2],
        m[0] * k[1] + m[1] * k[3],
        m[2] * k[0] + m[3] * k[2],
        m[2] * k[1] + m[3] * k[3],
    )


def plus(a, b):
    return tuple(x + y for x, y in zip(a, b))


def inverse(m):
    scale = 1.0 / (m[0] * m[3] - m[1] * m[2])
    return (m[3] * scale, -(m[1] * scale), -(m[2] * scale), m[0] * scale)


def interface(west, east, constant_only=False):
    _, _, _, lc, le, lw = unpack(west)
    fc, fe, fw, _, _, _ = unpack(east)
    loop = mat_mat(fw, le)
    inv = inverse((1.0 - loop[0], -loop[1], -loop[2], 1.0 - loop[3]))
    first_c = mat_vec(inv, plus(fc, mat_vec(fw, lc)))
    last_c = plus(lc, mat_vec(le, first_c))
    if constant_only:
        return first_c, last_c
    first_e = mat_mat(inv, fe)
    first_w = mat_mat(inv, mat_mat(fw, lw))
    last_e = mat_mat(le, first_e)
    last_w = plus(lw, mat_mat(le, first_w))
    return first_c, first_e, first_w, last_c, last_e, last_w


def joined(west, east):
    meet = interface(west, east)
    first_c, first_e, first_w, last_c, last_e, last_w = meet
    fc, fe, fw, _, _, _ = unpack(west)
    _, _, _, lc, le, lw = unpack(east)
    piece = (
        plus(fc, mat_vec(fe, first_c))
        + mat_mat(fe, first_e)
        + plus(fw, mat_mat(fe, first_w))
        + plus(lc, mat_vec(lw, last_c))
        + plus(le, mat_mat(lw, last_e))
        + mat_mat(lw, last_w)
    )
    return piece, sum(meet, ())


def rolled(values, by):
    count = values[0].shape[0]
    return tuple(pltpu.roll(x, by % count, 0) for x in values)


def split_pairs(meet, east, west, step):
    first = plus(plus(meet[0:2], mat_vec(meet[2:6], east)), mat_vec(meet[6:10], west))
    last = plus(plus(meet[10:12], mat_vec(meet[12:16], east)), mat_vec(meet[16:20], west))
    count = first[0].shape[0]
    place = lax.broadcasted_iota(jnp.int32, first[0].shape, 0)
    lower = lax.rem(place, 2 * step) < step
    if 2 * step < count:
        east = rolled(east, step)
    moved = rolled(last, step)
    return (
        tuple(jnp.where(lower, a, b) for a, b in zip(first, east)),
        tuple(jnp.where(lower, a, b) for a, b in zip(west, moved)),
    )


def kernel(
    peers, t_hbm, l2_hbm, l1_hbm, u1_hbm, u2_hbm, z_hbm,
    t_s, l2_s, l1_s, u1_s, u2_s, z_s, p_s, q_s, g_s, wa_s, wb_s,
    piece_s, inner_s, send_s, recv_s, back_s, ret_s,
    in_sem, out_sem, send_sem, recv_sem, back_send_sem, back_recv_sem,
):
    _, length, lines = t_hbm.shape
    tiles = lines // LANE
    pitch = t_s.shape[1]
    group = min(GROUP, tiles)
    me = lax.axis_index("lon")
    others = [lax.rem(me + k, peers) for k in range(1, peers)]

    def owning(who, action):
        if tiles < peers:
            pl.when(who < tiles)(action)
        else:
            action()

    def loads(tile, part):
        pairs = ((t_hbm, t_s), (l2_hbm, l2_s), (l1_hbm, l1_s), (u1_hbm, u1_s), (u2_hbm, u2_s))
        some = pl.ds(part * (length // PARTS), length // PARTS)
        return [
            pltpu.make_async_copy(
                src.at[:, some, pl.ds(tile * LANE, LANE)],
                dst.at[pl.ds(tile * SUB, SUB), some, :],
                in_sem.at[idx, tile, part],
            )
            for idx, (src, dst) in enumerate(pairs)
        ]

    flat_rows = (tiles + 1) * SUB * pitch
    t_f, l2_f, l1_f, u1_f, u2_f, z_f = (
        ref.reshape(flat_rows, LANE) for ref in (t_s, l2_s, l1_s, u1_s, u2_s, z_s)
    )

    def start_loads(base):
        for part in range(PARTS):
            for tile in range(base, base + group):
                for copy in loads(tile, part):
                    copy.start()

    start_loads(0)

    barrier = pltpu.get_barrier_semaphore()
    for peer in others:
        pl.semaphore_signal(
            barrier, inc=1, device_id={"lon": peer}, device_id_type=pl.DeviceIdType.MESH
        )

    ret_s[0] = jnp.zeros((SUB, LANE), F32)
    back_s[pl.ds(0, SUB), :] = jnp.ones((SUB, LANE), F32)
    zero = ret_s[0]
    one = back_s[pl.ds(0, SUB), :]

    def strided(tile, row):
        return pl.ds(tile * SUB * pitch + row, SUB, stride=pitch)

    def packed(tile):
        return pl.ds(tile * SUB, SUB)

    def outward(peer, source):
        return pltpu.make_async_remote_copy(
            src_ref=send_s.at[peer],
            dst_ref=recv_s.at[pl.ds(pl.multiple_of(source * SENT, SENT), SENT), :],
            send_sem=send_sem.at[peer],
            recv_sem=recv_sem.at[source],
            device_id={"lon": peer},
            device_id_type=pl.DeviceIdType.MESH,
        )

    def homeward(peer, source):
        return pltpu.make_async_remote_copy(
            src_ref=back_s.at[pl.ds(pl.multiple_of(peer * BACK, BACK), BACK), :],
            dst_ref=ret_s.at[source],
            send_sem=back_send_sem.at[peer],
            recv_sem=back_recv_sem.at[source],
            device_id={"lon": peer},
            device_id_type=pl.DeviceIdType.MESH,
        )

    def whole(tile, carry):
        piece = tuple(piece_s[tile, pl.ds(idx * SUB, SUB), :] for idx in range(20))
        for level in range(LEVELS):
            piece, meet = joined(piece, rolled(piece, -(1 << level)))
            for idx, value in enumerate(meet):
                inner_s[tile, pl.ds((level * 20 + idx) * SUB, SUB), :] = value
        for idx, value in enumerate(piece):
            send_s[tile, pl.ds(idx, 1), :] = value[0:1, :]
        return carry

    for base in range(0, tiles, group):
        members = list(range(base, base + group))

        def forward(i, state, members=members):
            new_state = []
            for tile, (p1, q1, g1, a1, b1, p2, q2, g2, a2, b2) in zip(members, state):
                here = strided(tile, i)
                l2, l1, u1, u2 = l2_f[here, :], l1_f[here, :], u1_f[here, :], u2_f[here, :]
                target = t_f[here, :]
                centre = (l2 + l1 + u1 + u2) - 1.0
                beta = l1 + l2 * p2
                scale = pl.reciprocal((centre - l2 * q2) - beta * p1, approx=True)
                p0 = (u1 + beta * q1) * scale
                q0 = u2 * scale
                far = l2 * scale
                near = beta * scale
                g0 = (far * g2 - target * scale) + near * g1
                a0 = far * a2 + near * a1
                b0 = far * b2 + near * b1
                at = packed(tile)
                p_s[i, at, :] = p0
                q_s[i, at, :] = q0
                g_s[i, at, :] = g0
                wa_s[i, at, :] = a0
                wb_s[i, at, :] = b0
                new_state.append((p0, q0, g0, a0, b0, p1, q1, g1, a1, b1))
            return tuple(new_state)

        start = (zero, zero, zero, zero, one, zero, zero, zero, one, zero)
        ends = (start,) * group
        for part in range(PARTS):
            for tile in members:
                for copy in loads(tile, part):
                    copy.wait()
            span = length // PARTS
            ends = lax.fori_loop(part * span, (part + 1) * span, forward, ends, unroll=min(8, span))
            if part == 0 and base + group < tiles:
                start_loads(base + group)

        def first_rows(i, state, members=members):
            new_state = []
            for tile, forms in zip(members, state):
                at = packed(tile)
                p, q, g = p_s[i, at, :], q_s[i, at, :], g_s[i, at, :]
                wa, wb = wa_s[i, at, :], wb_s[i, at, :]
                new_forms = []
                for c, x, y, a, b in forms:
                    new_forms.append((c + x * g, y + x * p, x * q, a + x * wa, b + x * wb))
                new_state.append(tuple(new_forms))
            return tuple(new_state)

        forms = ((zero, one, zero, zero, zero), (zero, zero, one, zero, zero))
        firsts = lax.fori_loop(0, length, first_rows, (forms,) * group, unroll=min(16, length))

        for tile, end, (f0, f1) in zip(members, ends, firsts):
            p1, q1, g1, a1, b1, p2, q2, g2, a2, b2 = end
            piece = (
                f0[0], f1[0],
                f0[1], f0[2], f1[1], f1[2],
                f0[3], f0[4], f1[3], f1[4],
                g2 + p2 * g1, g1,
                p2 * p1 + q2, p2 * q1, p1, q1,
                p2 * a1 + a2, p2 * b1 + b2, a1, b1,
            )
            for idx, value in enumerate(piece):
                piece_s[tile, pl.ds(idx * SUB, SUB), :] = value

        lax.fori_loop(base, base + group, whole, 0, unroll=2)
        if base == 0:
            pl.semaphore_wait(barrier, peers - 1)
        for tile in members:
            pl.when(me != tile)(lambda tile=tile: outward(tile, me).start())

    def solve_lines():
        recv_s[pl.ds(pl.multiple_of(me * SENT, SENT), SENT), :] = send_s[me]
        for peer in others:
            outward(me, peer).wait_recv()
        piece = tuple(recv_s[pl.ds(idx, peers, stride=SENT), :] for idx in range(20))
        meets = []
        step = 1
        while 2 * step < peers:
            piece, meet = joined(piece, rolled(piece, -step))
            meets.append(meet)
            step *= 2
        first, last = interface(piece, rolled(piece, -step), True)
        place = lax.broadcasted_iota(jnp.int32, (peers, LANE), 0)
        east = tuple(jnp.where(place < step, x, 0.0) for x in first)
        west = tuple(jnp.where(place < step, 0.0, x) for x in rolled(last, step))
        for meet in reversed(meets):
            step //= 2
            east, west = split_pairs(meet, east, west, step)
        for idx, value in enumerate(east + west):
            back_s[pl.ds(idx, peers, stride=BACK), :] = value
        for peer in others:
            homeward(peer, me).start()
        ret_s[me] = back_s[pl.ds(pl.multiple_of(me * BACK, BACK), BACK), :]

    owning(me, solve_lines)

    def store(tile, part):
        some = pl.ds(part * (length // PARTS), length // PARTS)
        return pltpu.make_async_copy(
            z_s.at[pl.ds(tile * SUB, SUB), some, :],
            z_hbm.at[:, some, pl.ds(tile * LANE, LANE)],
            out_sem.at[tile, part],
        )

    for base in range(0, tiles, group):
        members = list(range(base, base + group))
        start, bounds = [], []
        for tile in members:
            pl.when(me != tile)(lambda tile=tile: homeward(me, tile).wait_recv())
        for tile in members:
            e0, e1, w0, w1 = (
                jnp.broadcast_to(ret_s[tile, pl.ds(idx, 1), :], (SUB, LANE)) for idx in range(4)
            )
            east, west = (e0, e1), (w0, w1)
            for level in reversed(range(LEVELS)):
                meet = tuple(
                    inner_s[tile, pl.ds((level * 20 + idx) * SUB, SUB), :] for idx in range(20)
                )
                east, west = split_pairs(meet, east, west, 1 << level)
            start.append(east)
            bounds.append(west)

        def backward(step, state, members=members, bounds=bounds):
            i = length - 1 - step
            new_state = []
            for tile, (wa, wb), (x1, x2) in zip(members, bounds, state):
                at = packed(tile)
                free = (g_s[i, at, :] + wa_s[i, at, :] * wa) + wb_s[i, at, :] * wb
                x0 = (free + q_s[i, at, :] * x2) + p_s[i, at, :] * x1
                z_f[strided(tile, i), :] = 2.0 * x0 - t_f[strided(tile, i), :]
                new_state.append((x0, x1))
            return tuple(new_state)

        state = tuple(start)
        for part in reversed(range(PARTS)):
            span = length // PARTS
            done = (PARTS - 1 - part) * span
            state = lax.fori_loop(done, done + span, backward, state, unroll=min(16, span))
            for tile in members:
                store(tile, part).start()

    for tile in range(tiles):
        for part in range(PARTS):
            store(tile, part).wait()
    for tile in range(tiles):
        pl.when(me != tile)(lambda tile=tile: outward(tile, me).wait_send())

    def sent_home():
        for peer in others:
            homeward(peer, me).wait_send()

    owning(me, sent_home)


def per_device(tracer, lower2, lower1, upper1, upper2):
    rows, lines = tracer.shape
    peers = lax.axis_size("lon")
    tiles = lines // LANE
    assert rows % (PARTS * SUB * SUB) == 0 and peers & (peers - 1) == 0 and lines % LANE == 0 and tiles <= peers
    assert tiles % min(GROUP, tiles) == 0
    length = rows // SUB
    pitch = length if length % (2 * SUB) else length + SUB
    plane = pltpu.VMEM(((tiles + 1) * SUB, pitch, LANE), F32)
    factor = pltpu.VMEM((length, tiles * SUB, LANE), F32)
    sem = pltpu.SemaphoreType.DMA
    solved = pl.pallas_call(
        functools.partial(kernel, peers),
        out_shape=jax.ShapeDtypeStruct((SUB, length, lines), F32),
        in_specs=[pl.BlockSpec(memory_space=pl.ANY)] * 5,
        out_specs=pl.BlockSpec(memory_space=pl.ANY),
        scratch_shapes=[plane] * 6
        + [factor] * 5
        + [
            pltpu.VMEM((tiles, 20 * SUB, LANE), F32),
            pltpu.VMEM((tiles, LEVELS * 20 * SUB, LANE), F32),
            pltpu.VMEM((tiles, SENT, LANE), F32),
            pltpu.VMEM(((peers + 1) * SENT, LANE), F32),
            pltpu.VMEM(((peers + 1) * BACK, LANE), F32),
            pltpu.VMEM((tiles, BACK, LANE), F32),
            sem((5, tiles, PARTS)),
            sem((tiles, PARTS)),
            sem((peers,)),
            sem((peers,)),
            sem((peers,)),
            sem((peers,)),
        ],
        compiler_params=pltpu.CompilerParams(
            collective_id=0, has_side_effects=True, vmem_limit_bytes=50 * 1024 * 1024
        ),
        cost_estimate=pl.CostEstimate(
            flops=90 * rows * lines, bytes_accessed=24 * rows * lines, transcendentals=0
        ),
    )(*(x.reshape(SUB, length, lines) for x in (tracer, lower2, lower1, upper1, upper2)))
    return solved.reshape(rows, lines)


def solution(mesh):
    spec = P("lon", "lat")
    return jax.shard_map(
        per_device, mesh=mesh, in_specs=(spec,) * 5, out_specs=spec, check_vma=False
    )
```
